128 devices in a mesh: frow: 8 (over y, core), fcol: 16 (over x, z).
Axes of the slice: x: 4, y: 4, z: 4, core: 2. Of those that a mesh axis runs over, the one named last changes fastest.
Arguments:
- front_matrix: bfloat16 [28672, 28672], P('frow', 'fcol'), may hold values from -0.046875 to 0.046875
- test_matrix: bfloat16 [28672, 512], P('fcol'), may hold values from -6 to 6
- child_samples: bfloat16 [131072, 512], P(('frow', 'fcol')), may hold values from -6 to 6
- child_group: int32 [1024, 1], P(('frow', 'fcol')), may hold values from 0 to 7; in each aligned block of 8 rows (0 to 7, 8 to 15, ...) at most 4 rows name the same one
- child_block: int32 [1024], P(('frow', 'fcol')), may hold values from 0 to 27
- inv_leaf: bfloat16 [65536, 96], P(('frow', 'fcol')), may hold values from -0.25 to 0.25
- inv_parent: bfloat16 [32768, 64], P(('frow', 'fcol')), may hold values from -0.25 to 0.25
- pivot_leaf: int32 [128, 96], P(('frow', 'fcol')), may hold values from 0 to 223, as said below
- pivot_parent: int32 [128, 32], P(('frow', 'fcol')), may hold values from 0 to 191, as said below
Outputs:
- samples: bfloat16 [28672, 512], P(('frow', 'fcol'))
- interp_leaf: float32 [28672, 96], P(('frow', 'fcol'))
- interp_parent: float32 [12288, 64], P(('frow', 'fcol'))
- skeleton_parent: bfloat16 [4096, 512], P(('frow', 'fcol'))
The draws below stay inside these ranges and needn't reach their ends.
Inputs may be any that keep to these rules, and one draw needn't show every extreme that they name: `pivot_leaf`: within each leaf's row, 96 distinct values. `pivot_parent`: the two rows of leaves 2p and 2p+1 together hold 64 distinct values. `child_group`: among the 8 rows of one device, no group is named more than 4 times.
All inputs are finite; a program needn't handle non-finite values.
Results may differ from the reference program's by a relative error of at most 0.003.
Values may be sent and summed in bfloat16 or wider, within the bound.
No kernel may reach another device: no remote copies, remote signals or barrier semaphores. Data moves between devices by JAX's collectives and lax.ppermute only.
A program may use at most 128 MiB of HBM per device.

```python
import math
import jax
import jax.numpy as jnp
import numpy as np
from jax import lax

NF = 28672
S = 512
BLK = 128
K1 = 96
K2 = 64
CBD = 8
CAP = 4
NLEAF = 128
LEAF = 224
GB = 28
NCHILD = 1024
N_FROW = 8


def draw_pivot_leaf(key, part):
    key = jax.random.fold_in(key, 11)
    keys = jax.random.split(key, NLEAF)
    chosen = jax.vmap(lambda k: jax.random.permutation(k, LEAF)[:K1])(keys)
    return chosen.astype(jnp.int32)


def draw_pivot_parent(key, part):
    key = jax.random.fold_in(key, 12)
    keys = jax.random.split(key, NLEAF // 2)
    chosen = jax.vmap(lambda k: jax.random.permutation(k, 2 * K1)[:K2])(keys)
    return chosen.reshape(NLEAF, K2 // 2).astype(jnp.int32)


def set_ends(result, rng, least, high):
    shape = result.shape
    spot = [jax.random.randint(jax.random.fold_in(rng, axis), (), 0, shape[axis]) for axis in range(len(shape))]
    result = result.at[tuple(spot)].set(least)
    longest = shape.index(max(shape))
    spot[longest] = (spot[longest] + 1) % shape[longest]
    return result.at[tuple(spot)].set(high)


def strengthened(result, rng, source, target, parts, factor):
    owner, partner = [(jnp.arange(result.shape[axis_at]) // (result.shape[axis_at] // parts)).reshape([-1 if axis == axis_at else 1 for axis in range(result.ndim)]) for axis_at in (source, target)]
    chosen = jax.random.permutation(rng, parts)[partner]
    strong = (owner == chosen) | (owner == (partner + parts // 2) % parts)
    return jnp.where(strong, factor * result, result)


def level_of(own_key, shape, cuts, low, largest):
    gain = 1.0
    for dim, shards_of in cuts:
        heights = jax.random.uniform(jax.random.fold_in(jax.random.fold_in(own_key, 6), dim), (shards_of,), jnp.float32, low / len(cuts), largest / len(cuts))
        gain = gain * jnp.repeat(jnp.exp(heights), shape[dim] // shards_of).reshape((-1,) + (1,) * (len(shape) - 1 - dim))
    return gain


def routed_block(key, own, number, rows, amount, top, limit, slope):
    sequence = jax.random.permutation(key, amount)
    heavy_load, common = shares(amount, rows * top, limit, slope, True), shares(amount, rows * top, limit, slope, False)
    places = jnp.arange(amount)

    def named(lengths, offset_by):
        used = int((lengths > 0).sum())
        fixed = max(1, used // 4)
        passed = fixed + (places - fixed + offset_by * (used - fixed)) % max(1, amount - fixed)
        return jnp.zeros((amount,), jnp.int32).at[sequence[jnp.where(places < fixed, places, passed)]].set(jnp.asarray(lengths, jnp.int32))

    lengths = jnp.where(number % 4 == 0, named(heavy_load, number // 4), named(common, number - number // 4 - 1))
    mixed = jax.random.permutation(jax.random.fold_in(own, 3), amount)
    source_of, taker = mixed[0:amount // 2 * 2:2], mixed[1:amount // 2 * 2:2]
    slack = jnp.minimum(lengths[source_of] - 1, limit - lengths[taker]) // 2
    slack = jnp.where((source_of == sequence[0]) | (taker == sequence[0]) | (lengths[taker] == 0), 0, jnp.maximum(slack, 0))
    passed = jax.random.randint(jax.random.fold_in(own, 4), (amount // 2,), 0, 1 << 20) % (slack + 1)
    lengths = lengths.at[source_of].add(-passed).at[taker].add(passed)
    members = jnp.searchsorted(jnp.cumsum(lengths), jnp.arange(rows * top), side="right").astype(jnp.int32)
    table = members.reshape(top, rows).T
    table = table[jax.random.permutation(jax.random.fold_in(own, 1), rows)]
    offset_by = jax.random.randint(jax.random.fold_in(own, 2), (rows, 1), 0, top)
    return jnp.take_along_axis(table, (jnp.arange(top)[None, :] + offset_by) % top, axis=1)


def shares(number_of, total, bound, lean, full):
    weights = [(1 << 20) // math.isqrt(standing ** lean) + 1 for standing in range(1, number_of + 1)]
    largest = bound if full else min(bound, max(-(-total // number_of), total * weights[0] // sum(weights)))
    least = 1 if total - largest >= number_of - 1 else 0
    given, surplus = [largest] + [least] * (number_of - 1), total - largest - least * (number_of - 1)
    while surplus > 0:
        candidates = [i for i in range(1, number_of) if given[i] < largest] or [i for i in range(1, number_of) if given[i] < bound]
        pool, budget = sum([weights[i] for i in candidates]), surplus
        for i in candidates:
            addition = min(bound - given[i], max(1, budget * weights[i] // pool), surplus)
            given[i] = given[i] + addition
            surplus = surplus - addition
    return np.array(given)


def centred(rng, extent, scale, most, cuts=(), kind=jnp.bfloat16):
    gain = level_of(rng, extent, cuts, -0.22, 0.18) if cuts else 1.0
    array = jax.random.normal(rng, extent, jnp.float32) * scale * gain
    return jnp.minimum(jnp.maximum(array, -most), most).astype(kind)


def gaussian_with(rng, extent, width, reach, cuts, heavy, kind=jnp.bfloat16):
    array = width * jax.random.normal(rng, extent, jnp.float32)
    if cuts:
        array = array * level_of(rng, extent, cuts, -0.22, 0.18)
    return jnp.clip(strengthened(array, jax.random.fold_in(rng, 3), *heavy), -reach, reach).astype(kind)


def setup_inputs(seed: int = 0) -> dict:
    splits = jax.random.split(jax.random.key(seed), 10)
    front_matrix = gaussian_with(splits[0], (NF, NF), NF ** -0.5, 0.046875, ((0, 8), (1, 16)), (1, 0, 16, 2.0))
    test_matrix = centred(splits[1], (NF, S), 1.0, 6.0, ((0, 16),))
    child_samples = centred(splits[2], (NCHILD * BLK, S), 1.0, 6.0, ((0, 128),))
    child_group_keys = jax.random.split(jax.random.fold_in(splits[3], 1), NCHILD // CBD)
    child_group_turns = jax.random.permutation(jax.random.fold_in(splits[3], 3), NCHILD // CBD)
    child_group = jax.vmap(lambda own, number: routed_block(jax.random.fold_in(splits[3], 2), own, number, CBD, N_FROW, 1, CAP, 2))(child_group_keys, child_group_turns).reshape((NCHILD, 1))
    child_block = set_ends(jax.random.randint(splits[4], (NCHILD,), 0, GB), jax.random.fold_in(splits[4], 1), 0, GB - 1).astype(jnp.int32)
    inv_leaf = centred(splits[5], (NLEAF * S, K1), S ** -0.5, 0.25, ((0, 128),))
    inv_parent = centred(splits[6], (NLEAF * S // 2, K2), S ** -0.5, 0.25, ((0, 128),))
    pivot_leaf = draw_pivot_leaf(jax.random.fold_in(splits[9], 71), 0)
    pivot_parent = draw_pivot_parent(jax.random.fold_in(splits[9], 71), 0)
    return {"front_matrix": front_matrix, "test_matrix": test_matrix, "child_samples": child_samples, "child_group": child_group, "child_block": child_block, "inv_leaf": inv_leaf, "inv_parent": inv_parent, "pivot_leaf": pivot_leaf, "pivot_parent": pivot_parent}


def reference(front_matrix, test_matrix, child_samples, child_group, child_block, inv_leaf, inv_parent, pivot_leaf, pivot_parent):
    row_blocks = front_matrix.reshape(N_FROW, NF // N_FROW, NF)
    partial_value = lax.map(lambda rows: jnp.dot(rows, test_matrix, preferred_element_type=jnp.float32), row_blocks)
    partial_value = partial_value.reshape(NF, S)
    dest = (child_group[:, 0] * GB + child_block).astype(jnp.int32)
    placer = (jnp.arange(NF // BLK, dtype=jnp.int32)[:, None] == dest[None, :]).astype(jnp.float32)
    child_part = jnp.dot(placer, child_samples.reshape(NCHILD, BLK * S).astype(jnp.float32), preferred_element_type=jnp.float32)
    samples = (partial_value + child_part.reshape(NF, S)).astype(jnp.bfloat16)
    leaves = samples.reshape(NLEAF, LEAF, S)
    inverses = inv_leaf.reshape(NLEAF, S, K1).astype(jnp.float32)
    interp_leaf = jnp.einsum('nls,nsk->nlk', leaves.astype(jnp.float32), inverses).reshape(NF, K1)
    skeleton = jnp.take_along_axis(leaves, pivot_leaf[:, :, None], axis=1)
    stacked = skeleton.reshape(NLEAF // 2, 2 * K1, S)
    parents = inv_parent.reshape(NLEAF // 2, S, K2).astype(jnp.float32)
    interp_parent = jnp.einsum('pjs,psk->pjk', stacked.astype(jnp.float32), parents).reshape(NLEAF * K1, K2)
    chosen = pivot_parent.reshape(NLEAF // 2, K2)
    skeleton_parent = jnp.take_along_axis(stacked, chosen[:, :, None], axis=1).reshape(NLEAF * K2 // 2, S)
    return samples, interp_leaf, interp_parent, skeleton_parent
```

```python
import functools

import jax
import jax.numpy as jnp
from jax import lax
from jax.experimental import pallas as pl
from jax.experimental.pallas import tpu as pltpu
from jax.sharding import PartitionSpec as P

BF16 = jnp.bfloat16
F32 = jnp.float32
BLK = 128
CBD = 8
NX = 4
NZ = 4
NY = 4
UNIT = 32
COLS = 128
LOCAL = pl.BlockSpec(memory_space=pltpu.VMEM)
SCALAR = pl.BlockSpec(memory_space=pltpu.SMEM)
REMAIN = pl.BlockSpec(memory_space=pltpu.HBM)


def params(mebibytes):
    return pltpu.CompilerParams(vmem_limit_bytes=mebibytes * 1024 * 1024)


def cost(flops, moved_bytes):
    return pl.CostEstimate(flops=flops, bytes_accessed=moved_bytes, transcendentals=0)


def fetch(pairs, sems):
    copies = [pltpu.make_async_copy(src, dst, sems.at[i]) for i, (src, dst) in enumerate(pairs)]
    for copy in copies:
        copy.start()
    return copies


def front_kernel(pos, a_hbm, b_hbm, x1, x2, x3, x0, z1, z2, z3, z0, a, b, value, sems):
    half = a.shape[1]
    rows = half * UNIT
    pieces = [(b_hbm, b)]
    for i, shift in enumerate((1, 3, 2, 0)):
        pieces.append((a_hbm.at[:half, (pos[0] + shift) % NX], a.at[i]))
    for jr in range(NX):
        pieces.append((a_hbm.at[half:, jr], a.at[NX + jr]))
    copies = fetch(pieces, sems)
    copies[0].wait()

    def product(pair):
        for q in (2 * pair, 2 * pair + 1):
            copies[1 + q].wait()
        both = a[2 * pair : 2 * pair + 2].reshape(2 * rows, a.shape[-1])
        return jnp.dot(both, b[...], preferred_element_type=F32)

    for pair, outs in ((0, (x1, x3)), (1, (x2, x0))):
        value[...] = product(pair)
        for t, out in enumerate(outs):
            out[...] = value[t * rows : (t + 1) * rows].astype(out.dtype)
    for pair in (2, 3):
        value[...] = product(pair)
        for shift, out in ((1, z1), (2, z2), (3, z3), (0, z0)):
            at = pl.multiple_of((pos[1] + shift) % NZ * COLS, COLS)
            piece = value[:, pl.ds(at, COLS)].astype(out.dtype)
            out[2 * (pair - 2) : 2 * (pair - 1)] = piece.reshape(2, rows, COLS)


def front_products(pos, front, test):
    blocks, depth, cols = front.shape[0] // BLK, front.shape[1], test.shape[1]
    half = blocks // 2
    rows = half * UNIT
    shapes = [((rows, cols), t) for t in (BF16, BF16, BF16, F32)]
    shapes += [((NX, rows, COLS), t) for t in (BF16, BF16, BF16, F32)]
    return pl.pallas_call(
        front_kernel,
        out_shape=[jax.ShapeDtypeStruct(*s) for s in shapes],
        in_specs=[SCALAR, REMAIN, REMAIN],
        out_specs=[LOCAL] * 8,
        scratch_shapes=[
            pltpu.VMEM((2 * NX, half, UNIT, depth), BF16),
            pltpu.VMEM(test.shape, BF16),
            pltpu.VMEM((2 * rows, cols), F32),
            pltpu.SemaphoreType.DMA((2 * NX + 1,)),
        ],
        compiler_params=params(28),
        cost_estimate=cost(
            2 * front.size * cols, 2 * (front.size + test.size) + 5 * blocks * BLK * cols
        ),
        name="front",
    )(pos, front.reshape(blocks, NX, UNIT, depth), test)


def sum_kernel(pos, own, r1, r2, r3, to1, to2, to3, keep, *, axis):
    for shift, out in ((1, to1), (2, to2), (3, to3), (0, keep)):
        if axis == 0:
            at = (pos[0] + shift) % NX
        else:
            at = (slice(None), pl.ds(pl.multiple_of((pos[1] + shift) % NZ * COLS, COLS), COLS))
        out[...] = own[at] + r1[at].astype(F32) + r2[at].astype(F32) + r3[at].astype(F32)


def partial_sum(pos, own, arrived, axis):
    piece = (own.shape[-2], COLS)
    return pl.pallas_call(
        functools.partial(sum_kernel, axis=axis),
        out_shape=[jax.ShapeDtypeStruct(piece, F32)] * 4,
        in_specs=[SCALAR] + [LOCAL] * 4,
        out_specs=[LOCAL] * 4,
        compiler_params=params(8),
        cost_estimate=cost(3 * own.size, 14 * own.size),
        name="sum_z" if axis == 0 else "sum_x",
    )(pos, own, *arrived)


def pack_kernel(child, group, block, pivots, out, facts, sems, *, blocks):
    copies = fetch(
        [
            (child.at[:, x * UNIT : (x + 1) * UNIT, z * COLS : (z + 1) * COLS], out.at[x * NZ + z, :CBD])
            for x in range(NX)
            for z in range(NZ)
        ],
        sems,
    )
    facts[...] = jnp.zeros_like(facts)
    facts[0:1, : group.shape[1]] = (group[...] * blocks + block[...]).astype(F32)
    facts[1:2, : pivots.shape[1]] = pivots[...].astype(F32)
    told = facts[...].astype(BF16)
    for i in range(out.shape[0]):
        out[i, CBD] = told
    for copy in copies:
        copy.wait()


def pack(child, group, block, pivots, blocks):
    return pl.pallas_call(
        functools.partial(pack_kernel, blocks=blocks),
        out_shape=jax.ShapeDtypeStruct((NX * NZ, CBD + 1, UNIT, COLS), BF16),
        in_specs=[REMAIN] + [LOCAL] * 3,
        out_specs=LOCAL,
        scratch_shapes=[pltpu.VMEM((UNIT, COLS), F32), pltpu.SemaphoreType.DMA((NX * NZ,))],
        compiler_params=params(4),
        cost_estimate=cost(0, 4 * child.size),
        name="pack",
    )(child.reshape(CBD, BLK, child.shape[1]), group, block, pivots)


def place_kernel(pos, mine, other, to1, to2, to3, own, pivots, total, facts, told, slots, sems):
    blocks = own.shape[0]
    sources = mine.shape[0]
    for t, ref in ((0, mine), (1, other)):
        told[t * sources : (t + 1) * sources] = ref[:, CBD].astype(F32)
    dest = told[:, 0].astype(jnp.int32)
    group = dest // blocks
    facts[...] = jnp.where(
        group % 2 == pos[4], (group // 2 + NY - pos[3]) % NY * blocks + dest % blocks, NY * blocks
    )
    copy = pltpu.make_async_copy(facts, slots, sems.at[0])
    copy.start()
    pivots[...] = told[pl.ds(pos[2] // 2 * 2, 2), 1].astype(jnp.int32)
    total[...] = jnp.zeros_like(total)
    copy.wait()
    for t, ref in ((0, mine), (1, other)):
        def body(i, _, t=t, ref=ref):
            for j in range(CBD):
                at = slots[t * sources + i, j]
                total[at] += ref[i, j].astype(F32)
            return _

        lax.fori_loop(0, sources, body, 0)
    own[...] = total[:blocks]
    for shift, ref in ((1, to1), (2, to2), (3, to3)):
        ref[...] = total[shift * blocks : (shift + 1) * blocks].astype(BF16)


def place(pos, mine, other, blocks):
    piece = (blocks, UNIT, COLS)
    sources = mine.shape[0]
    return pl.pallas_call(
        place_kernel,
        out_shape=[jax.ShapeDtypeStruct(piece, BF16)] * 3
        + [jax.ShapeDtypeStruct(piece, F32), jax.ShapeDtypeStruct((2, COLS), jnp.int32)],
        in_specs=[SCALAR] + [LOCAL] * 2,
        out_specs=[LOCAL] * 5,
        scratch_shapes=[
            pltpu.VMEM((NY * blocks + 1, UNIT, COLS), F32),
            pltpu.VMEM((2 * sources, COLS), jnp.int32),
            pltpu.VMEM((2 * sources, UNIT, COLS), F32),
            pltpu.SMEM((2 * sources, COLS), jnp.int32),
            pltpu.SemaphoreType.DMA((1,)),
        ],
        compiler_params=params(8),
        cost_estimate=cost(16 * mine.size, 8 * mine.size),
        name="place",
    )(pos, mine, other)


def finish_kernel(pos, *refs):
    fx, fz, child, out, total = refs[:4], refs[4:8], refs[8:12], refs[12], refs[13]
    half = fx[0].shape[0]
    blocks = 2 * half
    for first, part in ((0, fx), (half, fz)):
        value = part[0][...] + part[1][...] + part[2][...] + part[3][...]
        span = slice(first, first + half)
        value = value + child[0][span] + child[1][span].astype(F32)
        value = value + child[2][span].astype(F32) + child[3][span].astype(F32)
        total[span] = value.astype(BF16)
    units = blocks * NX // out.shape[0]
    for leaf in range(out.shape[0]):
        offset = (pos[0] - units * leaf) % NX
        for slot in range(2):
            unit = units * leaf + offset + NX * slot
            value = total[jnp.minimum(unit // NX, blocks - 1)]
            for dest in (leaf // 2 * 2, leaf // 2 * 2 + 1):
                out[dest, leaf % 2, slot] = value


def finish(pos, fx, fz, child, leaves):
    blocks = child[0].shape[0]
    piece = (blocks // 2, UNIT, COLS)
    return pl.pallas_call(
        finish_kernel,
        out_shape=jax.ShapeDtypeStruct((leaves, 2, 2, UNIT, COLS), BF16),
        in_specs=[SCALAR] + [LOCAL] * 12,
        out_specs=LOCAL,
        scratch_shapes=[pltpu.VMEM(child[0].shape, BF16)],
        compiler_params=params(8),
        cost_estimate=cost(8 * child[0].size, 30 * child[0].size),
        name="finish",
    )(pos, *[f.reshape(piece) for f in fx], *[f.reshape(piece) for f in fz], *child)


def across(a, b):
    return lax.dot_general(a, b, (((1,), (1,)), ((), ())), preferred_element_type=F32)


def tail_kernel(pos, arrived, inv_leaf, inv_own, inv_other, piv_leaf, piv_parent,
                samples, interp_leaf, interp_parent, skeleton_parent, rows, stacked):
    leaf = pos[2]
    units = samples.shape[0] // UNIT
    parity = leaf % 2
    for x in range(NX):
        for z in range(NZ):
            for t in range(2):
                offset = (x - units * (leaf - parity + t)) % NX
                for slot in range(2):
                    rows[t, offset + NX * slot, :, z * COLS : (z + 1) * COLS] = arrived[x * NZ + z, t, slot]
    padded = rows.shape[1] * UNIT
    count = samples.shape[0]
    rank = interp_parent.shape[1]
    leaf_rows = rows[parity].reshape(padded, rows.shape[-1])
    samples[...] = leaf_rows[:count]
    interp_leaf[...] = across(inv_leaf[...], leaf_rows)[:, :count]

    def pick(pivots, source):
        hit = lax.broadcasted_iota(jnp.int32, (source.shape[0], pivots.shape[1]), 0) == pivots
        return lax.dot_general(
            hit.astype(F32).astype(BF16), source, (((0,), (0,)), ((), ())), preferred_element_type=F32
        ).astype(BF16)

    for t in range(2):
        stacked[t] = pick(piv_leaf[t : t + 1], rows[t].reshape(padded, rows.shape[-1]))
    both = stacked[...].reshape(2 * rank, stacked.shape[-1])
    skeleton_parent[...] = pick(piv_parent[...], both)
    depth = inv_own.shape[1]
    skeleton = stacked[parity]
    even = lax.select(parity == 0, inv_own[...], inv_other[...])
    odd = lax.select(parity == 0, inv_other[...], inv_own[...])
    interp_parent[...] = across(even, skeleton[:, :depth]) + across(odd, skeleton[:, depth:])


def tail(pos, arrived, inv_leaf, inv_own, inv_other, piv_leaf, piv_parent, count):
    rank, cols = inv_leaf.shape
    padded = 2 * NX * UNIT
    args = (arrived, inv_leaf, inv_own, inv_other, piv_leaf, piv_parent)
    outs = [
        jax.ShapeDtypeStruct((count, cols), BF16),
        jax.ShapeDtypeStruct((rank, count), F32),
        jax.ShapeDtypeStruct((inv_own.shape[0], rank), F32),
        jax.ShapeDtypeStruct((piv_parent.shape[1], cols), BF16),
    ]
    return pl.pallas_call(
        tail_kernel,
        out_shape=outs,
        in_specs=[SCALAR] + [LOCAL] * len(args),
        out_specs=[LOCAL] * len(outs),
        scratch_shapes=[
            pltpu.VMEM((2, padded // UNIT, UNIT, cols), BF16),
            pltpu.VMEM((2, rank, cols), BF16),
        ],
        compiler_params=params(8),
        cost_estimate=cost(6 * padded * rank * cols, 6 * padded * cols),
        name="tail",
    )(pos, *args)


def moved(x, axis, to):
    return lax.ppermute(x, axis, [(i, to(i)) for i in range(lax.axis_size(axis))])


def along_x(shift):
    return lambda i: (i + NZ * shift) % (NX * NZ)


def along_z(shift):
    return lambda i: i // NZ * NZ + (i + shift) % NZ


def along_y(shift):
    return lambda i: (i + 2 * shift) % (2 * NY)


def on_device(front, test, child, child_group, child_block, inv_leaf, inv_parent, pivot_leaf, pivot_parent):
    row, column = lax.axis_index("frow"), lax.axis_index("fcol")
    leaves = lax.axis_size("fcol")
    blocks = front.shape[0] // BLK
    rank = pivot_leaf.shape[1]
    pos = jnp.stack([column // NZ, column % NZ, column, row // 2, row % 2]).astype(jnp.int32)

    packed = pack(child, child_group.T, child_block.reshape(1, CBD), pivot_leaf, blocks)
    mine = lax.all_to_all(packed, "fcol", 0, 0, tiled=True)

    x1, x2, x3, own_x, z1, z2, z3, own_z = front_products(pos, front, test)
    in_x = [moved(v, "fcol", along_x(s)) for s, v in ((1, x1), (3, x3), (2, x2))]
    in_z = [moved(v, "fcol", along_z(s)) for s, v in ((1, z1), (3, z3), (2, z2))]
    mine, own_x, own_z = lax.optimization_barrier((mine, own_x, own_z))

    other = moved(mine, "frow", lambda i: i ^ 1)
    inv_other = moved(inv_parent.T, "fcol", lambda i: i ^ 1)

    *out_y, own_y, piv_leaf = place(pos, mine, other, blocks)
    piv_leaf = piv_leaf[:, :rank]
    in_y = [moved(v, "frow", along_y(s)) for s, v in zip((1, 2, 3), out_y)]

    *out_x, own_x = partial_sum(pos, own_x, in_x, 1)
    in_x = [moved(v, "fcol", along_z(s)) for s, v in zip((1, 2, 3), out_x)]
    *out_z, own_z = partial_sum(pos, own_z, in_z, 0)
    in_z = [moved(v, "fcol", along_x(s)) for s, v in zip((1, 2, 3), out_z)]

    placed = finish(pos, [own_x, *in_x], [own_z, *in_z], [own_y, *in_y], leaves)
    arrived = lax.all_to_all(placed, "fcol", 0, 0, tiled=True)
    count = front.shape[0] // leaves
    samples, interp_leaf, interp_parent, skeleton_parent = tail(
        pos, arrived, inv_leaf.T, inv_parent.T, inv_other, piv_leaf, pivot_parent, count
    )
    return samples, interp_leaf.T, interp_parent.T, skeleton_parent


def solution(mesh):
    both = P(("frow", "fcol"), None)
    return jax.shard_map(
        on_device,
        mesh=mesh,
        in_specs=(P("frow", "fcol"), P("fcol", None), both, both, P(("frow", "fcol")), both, both, both, both),
        out_specs=(both,) * 4,
        check_vma=False,
    )
```

```python
import functools

import jax
import jax.numpy as jnp
from jax import lax
from jax.experimental import pallas as pl
from jax.experimental.pallas import tpu as pltpu
from jax.sharding import PartitionSpec as P

BF16 = jnp.bfloat16
F32 = jnp.float32
BLK = 128
CBD = 8
NX = 4
NZ = 4
NY = 4
UNIT = 32
SCALE = 1
COLS = 128
LOCAL = pl.BlockSpec(memory_space=pltpu.VMEM)
REMAIN = pl.BlockSpec(memory_space=pltpu.HBM)
ANY = pl.BlockSpec(memory_space=pl.ANY)


def params(mebibytes):
    return pltpu.CompilerParams(vmem_limit_bytes=mebibytes * 1024 * 1024)


def cost(flops, moved_bytes):
    return pl.CostEstimate(flops=flops // SCALE, bytes_accessed=moved_bytes // SCALE, transcendentals=0)


def place_in_mesh():
    row, column = lax.axis_index("frow"), lax.axis_index("fcol")
    return column // NZ, column % NZ, column, row // 2, row % 2


def remote(value):
    return pltpu.with_memory_space_constraint(value, pltpu.HBM)


def fetch(pairs, sems):
    copies = [pltpu.make_async_copy(src, dst, sems.at[i]) for i, (src, dst) in enumerate(pairs)]
    for copy in copies:
        copy.start()
    return copies


def front_kernel(a_hbm, b_hbm, x0, x1, x3, xa, xb, z0, z1, z3, za, zb,
                 a, b, turned, value, sx0, sx1, sx3, sz0, sz1, sz3, sems, out_sems, *, cuts):
    x, z = place_in_mesh()[:2]
    half = a.shape[0] // 2
    spans = list(zip(cuts[:-1], cuts[1:]))
    copies = [pltpu.make_async_copy(b_hbm, b, sems.at[0])]
    copies += [pltpu.make_async_copy(a_hbm.at[lo:hi], a.at[lo:hi], sems.at[i + 1]) for i, (lo, hi) in enumerate(spans)]
    for copy in copies[:3]:
        copy.start()

    def arrive(i):
        copies[i].wait()
        if i + 3 < len(copies):
            copies[i + 3].start()

    stores = []

    def store(staged, out, at):
        copy = pltpu.make_async_copy(staged.at[at], out.at[at], out_sems.at[len(stores)])
        copy.start()
        stores.append(copy)

    arrive(0)
    for s in range(NZ):
        at = pl.multiple_of((z + s) % NZ * COLS, COLS)
        turned[:, s * COLS : (s + 1) * COLS] = b[:, pl.ds(at, COLS)]
    for i, (lo, hi) in enumerate(spans):
        arrive(i + 1)
        rows = (hi - lo) * BLK
        block = a[lo:hi].reshape(rows, a.shape[-1])
        product = jnp.dot(block, turned[...], preferred_element_type=F32)
        product = product.reshape(hi - lo, NX, UNIT, NZ * COLS)
        if hi <= half:
            value[: hi - lo] = product
            for s, staged, out in ((0, sx0, x0), (1, sx1, x1), (3, sx3, x3)):
                staged[lo:hi] = value[: hi - lo, (x + s) % NX]
                store(staged, out, pl.ds(lo, hi - lo))
            out, at = (xa, lo) if hi <= half // 2 else (xb, lo - half // 2)
            out[at : at + hi - lo] = value[: hi - lo, (x + 2) % NX].astype(BF16)
        else:
            for jr in range(NX):
                at = jr * half + lo - half
                piece = product[:, jr]
                for s, staged, out in ((0, sz0, z0), (1, sz1, z1), (3, sz3, z3)):
                    staged[at : at + hi - lo] = piece[..., s * COLS : (s + 1) * COLS]
                    store(staged, out, pl.ds(at, hi - lo))
                out, at = (za, at) if jr < NX // 2 else (zb, at - NX // 2 * half)
                out[at : at + hi - lo] = piece[..., 2 * COLS : 3 * COLS].astype(BF16)
    for copy in stores:
        copy.wait()


def inverse_tiles(shape):
    return [
        (slice(i, i + UNIT), slice(j, j + COLS))
        for i in range(0, shape[0], UNIT)
        for j in range(0, shape[1], COLS)
    ]


def front_products(front, test):
    blocks, depth, cols = front.shape[0] // BLK, front.shape[1], test.shape[1]
    half = blocks // 2
    step = half // 2
    cuts = (0, step // 2, *range(step, blocks + 1, step))
    kinds = ((1, F32), (1, F32), (1, F32), (2, BF16), (2, BF16))
    shapes = [((half // n, UNIT, cols), t) for n, t in kinds]
    shapes += [((NX * half // n, UNIT, COLS), t) for n, t in kinds]
    return pl.pallas_call(
        functools.partial(front_kernel, cuts=cuts),
        out_shape=[(pltpu.HBM if s[1] == F32 else jax.ShapeDtypeStruct)(*s) for s in shapes],
        in_specs=[REMAIN, REMAIN],
        out_specs=([REMAIN] * 3 + [LOCAL] * 2) * 2,
        scratch_shapes=[
            pltpu.VMEM((blocks, BLK, depth), BF16),
            pltpu.VMEM(test.shape, BF16),
            pltpu.VMEM(test.shape, BF16),
            pltpu.VMEM((step, NX, UNIT, cols), F32),
            *[pltpu.VMEM(*shape) for shape in shapes if shape[1] == F32],
            pltpu.SemaphoreType.DMA((len(cuts),)),
            pltpu.SemaphoreType.DMA((3 * (len(cuts) - 1 + 2 * NX),)),
        ],
        compiler_params=params(30),
        cost_estimate=cost(
            2 * front.size * cols, 2 * (front.size + test.size) + 5 * blocks * BLK * cols
        ),
        name="front",
    )(remote(front.reshape(blocks, BLK, depth)), remote(test))


def relay_kernel(hx1, hx3, xa, xb, hz1, hz3, za, zb, inverse, _, x_up, x_down, z_up, z_down, __,
                 x1, x3, z1, z3, sems):
    copies = fetch([(hx1, x1), (hx3, x3), (hz1, z1), (hz3, z3)], sems)
    for copy, own, part, out, at in zip(
        copies, (x1, x3, z1, z3), (xa, xb, za, zb), (x_up, x_down, z_up, z_down),
        (0, xa.shape[0], 0, za.shape[0]),
    ):
        copy.wait()
        half = part.shape[0]
        rest = half - at
        out[at : at + half] = (own[at : at + half] + part[...].astype(F32)).astype(BF16)
        out[rest : rest + half] = own[rest : rest + half].astype(BF16)
    for out in (z_up, z_down):
        for i, (rows, columns) in enumerate(inverse_tiles(inverse.shape)):
            out[z1.shape[0] + i] = inverse[rows, columns]


def relay(x1, x3, xa, xb, z1, z3, za, zb, inverse, mine):
    extra = len(inverse_tiles(inverse.shape))
    z_shape = (z1.shape[0] + extra, *z1.shape[1:])
    shapes = [x1.shape, x1.shape, z_shape, z_shape, mine.shape]
    return pl.pallas_call(
        relay_kernel,
        out_shape=[jax.ShapeDtypeStruct(shape, BF16) for shape in shapes],
        in_specs=([REMAIN] * 2 + [LOCAL] * 2) * 2 + [LOCAL] * 2,
        out_specs=[LOCAL] * 5,
        scratch_shapes=[
            *[pltpu.VMEM(v.shape, F32) for v in (x1, x3, z1, z3)],
            pltpu.SemaphoreType.DMA((4,)),
        ],
        input_output_aliases={9: 4},
        compiler_params=params(8),
        cost_estimate=cost(4 * x1.size, 14 * x1.size),
        name="relay",
    )(remote(x1), remote(x3), xa, xb, remote(z1), remote(z3), za, zb, inverse, mine)


def sum_x_kernel(held, r1, r2, token, to1, to2, to3, keep, own, sems):
    fetch([(held, own)], sems)[0].wait()
    for s, out in ((1, to1), (2, to2), (3, to3), (0, keep)):
        at = (slice(None), slice(None), slice(s * COLS, (s + 1) * COLS))
        out[...] = own[at] + r1[at].astype(F32) + r2[at].astype(F32)


def sum_z_kernel(held, r1, r2, token, to1, to2, to3, keep, inverse, own, sems):
    fetch([(held, own)], sems)[0].wait()
    x, z = place_in_mesh()[:2]
    half = keep.shape[0]
    for s, out in ((1, to1), (2, to2), (3, to3), (0, keep)):
        at = pl.ds((x + s) % NX * half, half)
        out[...] = own[at] + r1[at].astype(F32) + r2[at].astype(F32)
    for i, (rows, columns) in enumerate(inverse_tiles(inverse.shape)):
        inverse[rows, columns] = lax.select(z % 2 == 0, r2[NX * half + i], r1[NX * half + i])


def partial_sum(kernel, own, arrived, token, half, extra):
    piece = jax.ShapeDtypeStruct((half, UNIT, COLS), F32)
    outs = [piece] * 4 + extra
    return pl.pallas_call(
        kernel,
        out_shape=outs,
        in_specs=[REMAIN] + [LOCAL] * 2 + [ANY],
        out_specs=[LOCAL] * len(outs),
        scratch_shapes=[pltpu.VMEM(own.shape, F32), pltpu.SemaphoreType.DMA((1,))],
        compiler_params=params(8),
        cost_estimate=cost(3 * own.size, 14 * own.size),
        name=kernel.__name__[:5],
    )(remote(own), *arrived, token)


def pack_kernel(child, group_hbm, block_hbm, pivots_hbm, out, group, block, pivots, facts, sems, *, blocks):
    copies = fetch(
        [(group_hbm, group), (block_hbm, block), (pivots_hbm, pivots)]
        + [
            (child.at[:, x * UNIT : (x + 1) * UNIT, z * COLS : (z + 1) * COLS], out.at[x * NZ + z, :CBD])
            for x in range(NX)
            for z in range(NZ)
        ],
        sems,
    )
    facts[...] = jnp.zeros_like(facts)
    for copy in copies[:3]:
        copy.wait()
    facts[0:1, : group.shape[1]] = (group[...] * blocks + block[...]).astype(F32)
    facts[1:2, : pivots.shape[1]] = pivots[...].astype(F32)
    told = facts[...].astype(BF16)
    for i in range(out.shape[0]):
        out[i, CBD] = told
    for copy in copies[3:]:
        copy.wait()


def pack(child, group, block, pivots, blocks):
    return pl.pallas_call(
        functools.partial(pack_kernel, blocks=blocks),
        out_shape=jax.ShapeDtypeStruct((NX * NZ, CBD + 1, UNIT, COLS), BF16),
        in_specs=[REMAIN] * 4,
        out_specs=LOCAL,
        scratch_shapes=[
            *[pltpu.VMEM(v.shape, v.dtype) for v in (group, block, pivots)],
            pltpu.VMEM((UNIT, COLS), F32),
            pltpu.SemaphoreType.DMA((NX * NZ + 3,)),
        ],
        compiler_params=params(60),
        cost_estimate=cost(0, 4 * child.size),
        name="pack",
    )(child.reshape(CBD, BLK, child.shape[1]), group, block, pivots)


def place_kernel(mine, other, out, own, pivots, total, facts, told, slots, sems):
    pos = place_in_mesh()
    blocks = own.shape[0]
    sources = mine.shape[0]
    for t, ref in ((0, mine), (1, other)):
        told[t * sources : (t + 1) * sources] = ref[:, CBD].astype(F32)
    dest = told[:, 0].astype(jnp.int32)
    group = dest // blocks
    facts[...] = jnp.where(
        group % 2 == pos[4], group // 2 * blocks + dest % blocks, NY * blocks
    )
    copy = pltpu.make_async_copy(facts, slots, sems.at[0])
    copy.start()
    pivots[...] = told[pl.ds(pos[2] // 2 * 2, 2), 1].astype(jnp.int32)
    total[...] = jnp.zeros_like(total)
    copy.wait()
    for t, ref in ((0, mine), (1, other)):
        def body(i, _, t=t, ref=ref):
            for j in range(CBD):
                at = slots[t * sources + i, j]
                total[at] += ref[i, j].astype(F32)
            return _

        lax.fori_loop(0, sources, body, 0)
    own[...] = total[pl.ds(pos[3] * blocks, blocks)]
    out[...] = total[: NY * blocks].reshape(out.shape).astype(BF16)


def place(mine, other, blocks):
    piece = (blocks, UNIT, COLS)
    sources = mine.shape[0]
    return pl.pallas_call(
        place_kernel,
        out_shape=[
            jax.ShapeDtypeStruct((NY, *piece), BF16),
            jax.ShapeDtypeStruct(piece, F32),
            jax.ShapeDtypeStruct((2, COLS), jnp.int32),
        ],
        in_specs=[LOCAL] * 2,
        out_specs=[LOCAL] * 3,
        scratch_shapes=[
            pltpu.VMEM((NY * blocks + 1, UNIT, COLS), F32),
            pltpu.VMEM((2 * sources, COLS), jnp.int32),
            pltpu.VMEM((2 * sources, UNIT, COLS), F32),
            pltpu.SMEM((2 * sources, COLS), jnp.int32),
            pltpu.SemaphoreType.DMA((1,)),
        ],
        compiler_params=params(8),
        cost_estimate=cost(16 * mine.size, 8 * mine.size),
        name="place",
    )(mine, other)


def finish_kernel(*refs):
    pos = place_in_mesh()
    fx, fz, own, arrived, out, total = refs[:4], refs[4:8], *refs[8:12]
    half = fx[0].shape[0]
    blocks = 2 * half
    for first, part in ((0, fx), (half, fz)):
        value = part[0][...] + part[1][...] + part[2][...] + part[3][...]
        span = slice(first, first + half)
        value = value + own[span]
        for shift in (1, 2, 3):
            value = value + arrived[(pos[3] + shift) % NY, span].astype(F32)
        total[span] = value.astype(BF16)
    units = blocks * NX // out.shape[0]
    for leaf in range(out.shape[0]):
        offset = (pos[0] - units * leaf) % NX
        for slot in range(2):
            unit = units * leaf + offset + NX * slot
            value = total[jnp.minimum(unit // NX, blocks - 1)]
            for dest in (leaf // 2 * 2, leaf // 2 * 2 + 1):
                out[dest, leaf % 2, slot] = value


def finish(fx, fz, own, arrived, leaves):
    blocks = own.shape[0]
    piece = (blocks // 2, UNIT, COLS)
    return pl.pallas_call(
        finish_kernel,
        out_shape=jax.ShapeDtypeStruct((leaves, 2, 2, UNIT, COLS), BF16),
        in_specs=[LOCAL] * 10,
        out_specs=LOCAL,
        scratch_shapes=[pltpu.VMEM(own.shape, BF16)],
        compiler_params=params(8),
        cost_estimate=cost(8 * own.size, 30 * own.size),
        name="finish",
    )(*[f.reshape(piece) for f in fx], *[f.reshape(piece) for f in fz], own, arrived)


def across(a, b):
    return lax.dot_general(a, b, (((1,), (1,)), ((), ())), preferred_element_type=F32)


def tail_kernel(arrived, inv_leaf, inv_own, inv_other, piv_leaf, piv_parent,
                samples, interp_leaf, interp_parent, skeleton_parent, rows, stacked):
    pos = place_in_mesh()
    leaf = pos[2]
    units = samples.shape[0] // UNIT
    parity = leaf % 2
    for x in range(NX):
        for z in range(NZ):
            for t in range(2):
                offset = (x - units * (leaf - parity + t)) % NX
                for slot in range(2):
                    rows[t, offset + NX * slot, :, z * COLS : (z + 1) * COLS] = arrived[x * NZ + z, t, slot]
    padded = rows.shape[1] * UNIT
    count = samples.shape[0]
    rank = interp_parent.shape[1]
    leaf_rows = rows[parity].reshape(padded, rows.shape[-1])
    samples[...] = leaf_rows[:count]
    interp_leaf[...] = across(inv_leaf[...], leaf_rows)[:, :count]

    def pick(pivots, source):
        hit = lax.broadcasted_iota(jnp.int32, (source.shape[0], pivots.shape[1]), 0) == pivots
        return lax.dot_general(
            hit.astype(F32).astype(BF16), source, (((0,), (0,)), ((), ())), preferred_element_type=F32
        ).astype(BF16)

    for t in range(2):
        stacked[t] = pick(piv_leaf[t : t + 1], rows[t].reshape(padded, rows.shape[-1]))
    both = stacked[...].reshape(2 * rank, stacked.shape[-1])
    skeleton_parent[...] = pick(piv_parent[...], both)
    depth = inv_own.shape[1]
    skeleton = stacked[parity]
    even = lax.select(parity == 0, inv_own[...], inv_other[...])
    odd = lax.select(parity == 0, inv_other[...], inv_own[...])
    interp_parent[...] = across(even, skeleton[:, :depth]) + across(odd, skeleton[:, depth:])


def tail(arrived, inv_leaf, inv_own, inv_other, piv_leaf, piv_parent, count):
    rank, cols = inv_leaf.shape
    padded = 2 * NX * UNIT
    args = (arrived, inv_leaf, inv_own, inv_other, piv_leaf, piv_parent)
    outs = [
        jax.ShapeDtypeStruct((count, cols), BF16),
        jax.ShapeDtypeStruct((rank, count), F32),
        jax.ShapeDtypeStruct((inv_own.shape[0], rank), F32),
        jax.ShapeDtypeStruct((piv_parent.shape[1], cols), BF16),
    ]
    return pl.pallas_call(
        tail_kernel,
        out_shape=outs,
        in_specs=[LOCAL] * len(args),
        out_specs=[LOCAL] * len(outs),
        scratch_shapes=[
            pltpu.VMEM((2, padded // UNIT, UNIT, cols), BF16),
            pltpu.VMEM((2, rank, cols), BF16),
        ],
        compiler_params=params(8),
        cost_estimate=cost(6 * padded * rank * cols, 6 * padded * cols),
        name="tail",
    )(*args)


def moved(x, axis, to):
    return lax.ppermute(x, axis, [(i, to(i)) for i in range(lax.axis_size(axis))])


def along_x(shift):
    return lambda i: (i + NZ * shift) % (NX * NZ)


def along_z(shift):
    return lambda i: i // NZ * NZ + (i + shift) % NZ


def on_device(front, test, child, child_group, child_block, inv_leaf, inv_parent, pivot_leaf, pivot_parent):
    row, column = lax.axis_index("frow"), lax.axis_index("fcol")
    leaves = lax.axis_size("fcol")
    blocks = front.shape[0] // BLK
    rank = pivot_leaf.shape[1]

    packed = pack(child, child_group.T, child_block.reshape(1, CBD), pivot_leaf, blocks)
    mine = lax.all_to_all(packed, "fcol", 0, 0, tiled=True)

    own_x, x1, x3, xa, xb, own_z, z1, z3, za, zb = front_products(front, test)
    xa, xb = moved(xa, "fcol", along_x(1)), moved(xb, "fcol", along_x(3))
    za, zb = moved(za, "fcol", along_z(1)), moved(zb, "fcol", along_z(3))
    x_up, x_down, z_up, z_down, mine = relay(x1, x3, xa, xb, z1, z3, za, zb, inv_parent.T, mine)
    other = moved(mine, "frow", lambda i: i ^ 1)
    in_x = [moved(x_up, "fcol", along_x(1)), moved(x_down, "fcol", along_x(3))]
    in_z = [moved(z_up, "fcol", along_z(1)), moved(z_down, "fcol", along_z(3))]

    out_y, own_y, piv_leaf = place(mine, other, blocks)
    in_y = lax.all_to_all(
        out_y, "frow", 0, 0, tiled=True, axis_index_groups=[[2 * i + core for i in range(NY)] for core in range(2)]
    )
    token, piv_leaf = piv_leaf, piv_leaf[:, :rank]

    half = blocks // 2
    *out_x, own_x = partial_sum(sum_x_kernel, own_x, in_x, token, half, [])
    in_x = [moved(v, "fcol", along_z(s)) for s, v in zip((1, 2, 3), out_x)]
    inverse = jax.ShapeDtypeStruct(inv_parent.T.shape, BF16)
    *out_z, own_z, inv_other = partial_sum(sum_z_kernel, own_z, in_z, token, half, [inverse])
    in_z = [moved(v, "fcol", along_x(s)) for s, v in zip((1, 2, 3), out_z)]

    placed = finish([own_x, *in_x], [own_z, *in_z], own_y, in_y, leaves)
    arrived = lax.all_to_all(placed, "fcol", 0, 0, tiled=True)
    count = front.shape[0] // leaves
    samples, interp_leaf, interp_parent, skeleton_parent = tail(
        arrived, inv_leaf.T, inv_parent.T, inv_other, piv_leaf, pivot_parent, count
    )
    return samples, interp_leaf.T, interp_parent.T, skeleton_parent


def solution(mesh):
    both = P(("frow", "fcol"), None)
    return jax.shard_map(
        on_device,
        mesh=mesh,
        in_specs=(P("frow", "fcol"), P("fcol", None), both, both, P(("frow", "fcol")), both, both, both, both),
        out_specs=(both,) * 4,
        check_vma=False,
    )
```

```python
import functools

import jax
import jax.numpy as jnp
from jax import lax
from jax.experimental import pallas as pl
from jax.experimental.pallas import tpu as pltpu
from jax.sharding import PartitionSpec as P

BF16 = jnp.bfloat16
F32 = jnp.float32
BLK = 128
CBD = 8
NX = 4
NZ = 4
NY = 4
UNIT = 32
SCALE = 1
COLS = 128
LOCAL = pl.BlockSpec(memory_space=pltpu.VMEM)
REMAIN = pl.BlockSpec(memory_space=pltpu.HBM)
ANY = pl.BlockSpec(memory_space=pl.ANY)


def params(mebibytes):
    return pltpu.CompilerParams(vmem_limit_bytes=mebibytes * 1024 * 1024)


def cost(flops, moved_bytes):
    return pl.CostEstimate(flops=flops // SCALE, bytes_accessed=moved_bytes // SCALE, transcendentals=0)


def place_in_mesh():
    row, column = lax.axis_index("frow"), lax.axis_index("fcol")
    return column // NZ, column % NZ, column, row // 2, row % 2


def remote(value):
    return pltpu.with_memory_space_constraint(value, pltpu.HBM)


def fetch(pairs, sems):
    copies = [pltpu.make_async_copy(src, dst, sems.at[i]) for i, (src, dst) in enumerate(pairs)]
    for copy in copies:
        copy.start()
    return copies


def front_kernel(a_hbm, b_hbm, x0, x1, x3, u1, u3, xa, xb, z0, z1, z3, w1, w3, za, zb,
                 a, b, turned, value, sx0, sx1, sx3, su1, su3, sz0, sz1, sz3, sw1, sw3, sems, out_sems, *, cuts):
    x, z = place_in_mesh()[:2]
    half = a.shape[0] // 2
    spans = list(zip(cuts[:-1], cuts[1:]))
    copies = [pltpu.make_async_copy(b_hbm, b, sems.at[0])]
    copies += [pltpu.make_async_copy(a_hbm.at[lo:hi], a.at[lo:hi], sems.at[i + 1]) for i, (lo, hi) in enumerate(spans)]
    for copy in copies[:3]:
        copy.start()

    def arrive(i):
        copies[i].wait()
        if i + 3 < len(copies):
            copies[i + 3].start()

    stores = []

    def store(staged, out, at):
        copy = pltpu.make_async_copy(staged.at[at], out.at[at], out_sems.at[len(stores)])
        copy.start()
        stores.append(copy)

    arrive(0)
    for s in range(NZ):
        at = pl.multiple_of((z + s) % NZ * COLS, COLS)
        turned[:, s * COLS : (s + 1) * COLS] = b[:, pl.ds(at, COLS)]
    for i, (lo, hi) in enumerate(spans):
        arrive(i + 1)
        rows = (hi - lo) * BLK
        block = a[lo:hi].reshape(rows, a.shape[-1])
        product = jnp.dot(block, turned[...], preferred_element_type=F32)
        product = product.reshape(hi - lo, NX, UNIT, NZ * COLS)
        if hi <= half:
            value[: hi - lo] = product
            first = hi <= half // 2
            at = lo if first else lo - half // 2
            one, three, two = ((sx1, x1), (su3, u3), xa) if first else ((su1, u1), (sx3, x3), xb)
            for s, (staged, out), start in ((0, (sx0, x0), lo), (1, one, at), (3, three, at)):
                staged[start : start + hi - lo] = value[: hi - lo, (x + s) % NX].astype(staged.dtype)
                store(staged, out, pl.ds(start, hi - lo))
            two[at : at + hi - lo] = value[: hi - lo, (x + 2) % NX].astype(BF16)
        else:
            for jr in range(NX):
                at = jr * half + lo - half
                piece = product[:, jr]
                first = jr < NX // 2
                near = at if first else at - NX // 2 * half
                one, three, two = ((sz1, z1), (sw3, w3), za) if first else ((sw1, w1), (sz3, z3), zb)
                for s, (staged, out), start in ((0, (sz0, z0), at), (1, one, near), (3, three, near)):
                    staged[start : start + hi - lo] = piece[..., s * COLS : (s + 1) * COLS].astype(staged.dtype)
                    store(staged, out, pl.ds(start, hi - lo))
                two[near : near + hi - lo] = piece[..., 2 * COLS : 3 * COLS].astype(BF16)
    for copy in stores:
        copy.wait()


def inverse_tiles(shape):
    return [
        (slice(i, i + UNIT), slice(j, j + COLS))
        for i in range(0, shape[0], UNIT)
        for j in range(0, shape[1], COLS)
    ]


def front_products(front, test):
    blocks, depth, cols = front.shape[0] // BLK, front.shape[1], test.shape[1]
    half = blocks // 2
    step = half // 2
    cuts = (0, step // 2, *range(step, blocks + 1, step))
    kinds = ((1, F32), (2, F32), (2, F32), (2, BF16), (2, BF16), (2, BF16), (2, BF16))
    shapes = [((half // n, UNIT, cols), t) for n, t in kinds]
    shapes += [((NX * half // n, UNIT, COLS), t) for n, t in kinds]
    later = [i % 7 < 5 for i in range(14)]
    return pl.pallas_call(
        functools.partial(front_kernel, cuts=cuts),
        out_shape=[(pltpu.HBM if l else jax.ShapeDtypeStruct)(*s) for s, l in zip(shapes, later)],
        in_specs=[REMAIN, REMAIN],
        out_specs=[REMAIN if l else LOCAL for l in later],
        scratch_shapes=[
            pltpu.VMEM((blocks, BLK, depth), BF16),
            pltpu.VMEM(test.shape, BF16),
            pltpu.VMEM(test.shape, BF16),
            pltpu.VMEM((step, NX, UNIT, cols), F32),
            *[pltpu.VMEM(*s) for s, l in zip(shapes, later) if l],
            pltpu.SemaphoreType.DMA((len(cuts),)),
            pltpu.SemaphoreType.DMA((3 * (len(cuts) - 1 + 2 * NX),)),
        ],
        compiler_params=params(30),
        cost_estimate=cost(
            2 * front.size * cols, 2 * (front.size + test.size) + 5 * blocks * BLK * cols
        ),
        name="front",
    )(remote(front.reshape(blocks, BLK, depth)), remote(test))


def relay_kernel(hx1, hx3, hu1, hu3, xa, xb, hz1, hz3, hw1, hw3, za, zb, inverse, _,
                 x_up, x_down, z_up, z_down, __, x1, x3, z1, z3, sems):
    nx, nz = x1.shape[0], z1.shape[0]
    copies = fetch(
        [
            (hx1, x1), (hx3, x3), (hz1, z1), (hz3, z3),
            (hu1, x_up.at[nx : 2 * nx]), (hu3, x_down.at[:nx]),
            (hw1, z_up.at[nz : 2 * nz]), (hw3, z_down.at[:nz]),
        ],
        sems,
    )
    for out in (z_up, z_down):
        for i, (rows, columns) in enumerate(inverse_tiles(inverse.shape)):
            out[2 * nz + i] = inverse[rows, columns]
    for copy, own, part, out, at in zip(
        copies, (x1, x3, z1, z3), (xa, xb, za, zb), (x_up, x_down, z_up, z_down), (0, nx, 0, nz)
    ):
        copy.wait()
        out[at : at + own.shape[0]] = (own[...] + part[...].astype(F32)).astype(BF16)
    for copy in copies[4:]:
        copy.wait()


def relay(x_parts, xa, xb, z_parts, za, zb, inverse, mine):
    extra = len(inverse_tiles(inverse.shape))
    nx, nz = xa.shape[0], za.shape[0]
    x_shape, z_shape = (2 * nx, *xa.shape[1:]), (2 * nz + extra, *za.shape[1:])
    shapes = [x_shape, x_shape, z_shape, z_shape, mine.shape]
    return pl.pallas_call(
        relay_kernel,
        out_shape=[jax.ShapeDtypeStruct(shape, BF16) for shape in shapes],
        in_specs=([REMAIN] * 4 + [LOCAL] * 2) * 2 + [LOCAL] * 2,
        out_specs=[LOCAL] * 5,
        scratch_shapes=[
            *[pltpu.VMEM(v.shape, F32) for v in (xa, xb, za, zb)],
            pltpu.SemaphoreType.DMA((8,)),
        ],
        input_output_aliases={13: 4},
        compiler_params=params(8),
        cost_estimate=cost(4 * xa.size, 28 * xa.size),
        name="relay",
    )(*map(remote, x_parts), xa, xb, *map(remote, z_parts), za, zb, inverse, mine)


def sum_x_kernel(held, r1, r2, token, to1, to2, to3, keep, own, sems):
    outs = ((1, to1), (2, to2), (3, to3), (0, keep))
    spans = [(slice(None), slice(None), slice(s * COLS, (s + 1) * COLS)) for s, _ in outs]
    copies = fetch([(held.at[at], own.at[at]) for at in spans], sems)
    for at, copy, (_, out) in zip(spans, copies, outs):
        copy.wait()
        out[...] = (own[at] + r1[at].astype(F32) + r2[at].astype(F32)).astype(out.dtype)


def sum_z_kernel(held, r1, r2, token, to1, to2, to3, keep, inverse, own, sems):
    x, z = place_in_mesh()[:2]
    half = keep.shape[0]
    outs = ((1, to1), (2, to2), (3, to3), (0, keep))
    spans = [pl.ds((x + s) % NX * half, half) for s, _ in outs]
    copies = fetch([(held.at[at], own.at[at]) for at in spans], sems)
    for at, copy, (_, out) in zip(spans, copies, outs):
        copy.wait()
        out[...] = (own[at] + r1[at].astype(F32) + r2[at].astype(F32)).astype(out.dtype)
    for i, (rows, columns) in enumerate(inverse_tiles(inverse.shape)):
        inverse[rows, columns] = lax.select(z % 2 == 0, r2[NX * half + i], r1[NX * half + i])


def partial_sum(kernel, own, arrived, token, half, extra):
    outs = [jax.ShapeDtypeStruct((half, UNIT, COLS), t) for t in (F32, BF16, F32, F32)] + extra
    return pl.pallas_call(
        kernel,
        out_shape=outs,
        in_specs=[REMAIN] + [LOCAL] * 2 + [ANY],
        out_specs=[LOCAL] * len(outs),
        scratch_shapes=[pltpu.VMEM(own.shape, F32), pltpu.SemaphoreType.DMA((4,))],
        compiler_params=params(8),
        cost_estimate=cost(3 * own.size, 14 * own.size),
        name=kernel.__name__[:5],
    )(remote(own), *arrived, token)


def pack_kernel(child, group_hbm, block_hbm, pivots_hbm, out, group, block, pivots, facts, local, sems, *, blocks):
    copies = fetch(
        [(group_hbm, group), (block_hbm, block), (pivots_hbm, pivots)]
        + [(child.at[i : i + 2], local.at[i : i + 2]) for i in range(0, CBD, 2)],
        sems,
    )
    facts[...] = jnp.zeros_like(facts)
    for copy in copies[:3]:
        copy.wait()
    facts[0:1, : group.shape[1]] = (group[...] * blocks + block[...]).astype(F32)
    facts[1:2, : pivots.shape[1]] = pivots[...].astype(F32)
    told = facts[...].astype(BF16)
    for i in range(out.shape[0]):
        out[i, CBD] = told
    for i in range(0, CBD, 2):
        copies[3 + i // 2].wait()
        for x in range(NX):
            for z in range(NZ):
                part = local[i : i + 2, x * UNIT : (x + 1) * UNIT, z * COLS : (z + 1) * COLS]
                out[x * NZ + z, i : i + 2] = part


def pack(child, group, block, pivots, blocks):
    child = remote(child.reshape(CBD, BLK, child.shape[1]))
    return pl.pallas_call(
        functools.partial(pack_kernel, blocks=blocks),
        out_shape=jax.ShapeDtypeStruct((NX * NZ, CBD + 1, UNIT, COLS), BF16),
        in_specs=[REMAIN] * 4,
        out_specs=LOCAL,
        scratch_shapes=[
            *[pltpu.VMEM(v.shape, v.dtype) for v in (group, block, pivots)],
            pltpu.VMEM((UNIT, COLS), F32),
            pltpu.VMEM(child.shape, BF16),
            pltpu.SemaphoreType.DMA((CBD // 2 + 3,)),
        ],
        compiler_params=params(60),
        cost_estimate=cost(0, 4 * child.size),
        name="pack",
    )(child, group, block, pivots)


def place_kernel(mine, other, out, own, pivots, total, facts, told, slots, sems):
    pos = place_in_mesh()
    blocks = out.shape[1]
    sources = mine.shape[0]
    for t, ref in ((0, mine), (1, other)):
        told[t * sources : (t + 1) * sources] = ref[:, CBD].astype(F32)
    dest = told[:, 0].astype(jnp.int32)
    group = dest // blocks
    facts[...] = jnp.where(
        group % 2 == pos[4], group // 2 * blocks + dest % blocks, NY * blocks
    )
    copy = pltpu.make_async_copy(facts, slots, sems.at[0])
    copy.start()
    pivots[...] = told[pl.ds(pos[2] // 2 * 2, 2), 1].astype(jnp.int32)
    total[...] = jnp.zeros_like(total)
    copy.wait()
    for t, ref in ((0, mine), (1, other)):
        def body(i, _, t=t, ref=ref):
            for j in range(CBD):
                at = slots[t * sources + i, j]
                total[at] += ref[i, j].astype(F32)
            return _

        lax.fori_loop(0, sources, body, 0)
    keep = pltpu.make_async_copy(total.at[pl.ds(pos[3] * blocks, blocks)], own, sems.at[0])
    keep.start()
    out[...] = total[: NY * blocks].reshape(out.shape).astype(BF16)
    keep.wait()


def place(mine, other, blocks):
    piece = (blocks, UNIT, COLS)
    sources = mine.shape[0]
    return pl.pallas_call(
        place_kernel,
        out_shape=[
            jax.ShapeDtypeStruct((NY, *piece), BF16),
            pltpu.HBM(piece, F32),
            jax.ShapeDtypeStruct((2, COLS), jnp.int32),
        ],
        in_specs=[LOCAL] * 2,
        out_specs=[LOCAL, REMAIN, LOCAL],
        scratch_shapes=[
            pltpu.VMEM((NY * blocks + 1, UNIT, COLS), F32),
            pltpu.VMEM((2 * sources, COLS), jnp.int32),
            pltpu.VMEM((2 * sources, UNIT, COLS), F32),
            pltpu.SMEM((2 * sources, COLS), jnp.int32),
            pltpu.SemaphoreType.DMA((1,)),
        ],
        compiler_params=params(8),
        cost_estimate=cost(16 * mine.size, 8 * mine.size),
        name="place",
    )(mine, other)


def finish_kernel(*refs):
    pos = place_in_mesh()
    fx, fz, held, arrived, out, total, own, sems = refs[:4], refs[4:8], *refs[8:14]
    fetched = fetch([(held, own)], sems)[0]
    half = fx[0].shape[0]
    blocks = 2 * half
    for first, part in ((0, fx), (half, fz)):
        value = part[0][...] + part[1][...] + part[2][...].astype(F32) + part[3][...]
        span = slice(first, first + half)
        if first == 0:
            fetched.wait()
        value = value + own[span]
        for shift in (1, 2, 3):
            value = value + arrived[(pos[3] + shift) % NY, span].astype(F32)
        total[span] = value.astype(BF16)
    units = blocks * NX // out.shape[0]
    for leaf in range(out.shape[0]):
        offset = (pos[0] - units * leaf) % NX
        for slot in range(2):
            unit = units * leaf + offset + NX * slot
            value = total[jnp.minimum(unit // NX, blocks - 1)]
            for dest in (leaf // 2 * 2, leaf // 2 * 2 + 1):
                out[dest, leaf % 2, slot] = value


def finish(fx, fz, own, arrived, leaves):
    blocks = own.shape[0]
    piece = (blocks // 2, UNIT, COLS)
    return pl.pallas_call(
        finish_kernel,
        out_shape=jax.ShapeDtypeStruct((leaves, 2, 2, UNIT, COLS), BF16),
        in_specs=[LOCAL] * 8 + [REMAIN, LOCAL],
        out_specs=LOCAL,
        scratch_shapes=[
            pltpu.VMEM(own.shape, BF16),
            pltpu.VMEM(own.shape, F32),
            pltpu.SemaphoreType.DMA((1,)),
        ],
        compiler_params=params(8),
        cost_estimate=cost(8 * own.size, 30 * own.size),
        name="finish",
    )(*[f.reshape(piece) for f in fx], *[f.reshape(piece) for f in fz], remote(own), arrived)


def across(a, b):
    return lax.dot_general(a, b, (((1,), (1,)), ((), ())), preferred_element_type=F32)


def tail_kernel(arrived, inv_leaf, inv_own, inv_other, piv_leaf, piv_parent,
                samples, interp_leaf, interp_parent, skeleton_parent, rows, stacked):
    pos = place_in_mesh()
    leaf = pos[2]
    units = samples.shape[0] // UNIT
    parity = leaf % 2
    for x in range(NX):
        for z in range(NZ):
            for t in range(2):
                offset = (x - units * (leaf - parity + t)) % NX
                for slot in range(2):
                    rows[t, offset + NX * slot, :, z * COLS : (z + 1) * COLS] = arrived[x * NZ + z, t, slot]
    padded = rows.shape[1] * UNIT
    count = samples.shape[0]
    rank = interp_parent.shape[1]
    leaf_rows = rows[parity].reshape(padded, rows.shape[-1])
    samples[...] = leaf_rows[:count]
    interp_leaf[...] = across(inv_leaf[...], leaf_rows)[:, :count]

    def pick(pivots, source):
        hit = lax.broadcasted_iota(jnp.int32, (source.shape[0], pivots.shape[1]), 0) == pivots
        return lax.dot_general(
            hit.astype(F32).astype(BF16), source, (((0,), (0,)), ((), ())), preferred_element_type=F32
        ).astype(BF16)

    for t in range(2):
        stacked[t] = pick(piv_leaf[t : t + 1], rows[t].reshape(padded, rows.shape[-1]))
    both = stacked[...].reshape(2 * rank, stacked.shape[-1])
    skeleton_parent[...] = pick(piv_parent[...], both)
    depth = inv_own.shape[1]
    skeleton = stacked[parity]
    even = lax.select(parity == 0, inv_own[...], inv_other[...])
    odd = lax.select(parity == 0, inv_other[...], inv_own[...])
    interp_parent[...] = across(even, skeleton[:, :depth]) + across(odd, skeleton[:, depth:])


def tail(arrived, inv_leaf, inv_own, inv_other, piv_leaf, piv_parent, count):
    rank, cols = inv_leaf.shape
    padded = 2 * NX * UNIT
    args = (arrived, inv_leaf, inv_own, inv_other, piv_leaf, piv_parent)
    outs = [
        jax.ShapeDtypeStruct((count, cols), BF16),
        jax.ShapeDtypeStruct((rank, count), F32),
        jax.ShapeDtypeStruct((inv_own.shape[0], rank), F32),
        jax.ShapeDtypeStruct((piv_parent.shape[1], cols), BF16),
    ]
    return pl.pallas_call(
        tail_kernel,
        out_shape=outs,
        in_specs=[LOCAL] * len(args),
        out_specs=[LOCAL] * len(outs),
        scratch_shapes=[
            pltpu.VMEM((2, padded // UNIT, UNIT, cols), BF16),
            pltpu.VMEM((2, rank, cols), BF16),
        ],
        compiler_params=params(8),
        cost_estimate=cost(6 * padded * rank * cols, 6 * padded * cols),
        name="tail",
    )(*args)


def moved(x, axis, to):
    return lax.ppermute(x, axis, [(i, to(i)) for i in range(lax.axis_size(axis))])


def along_x(shift):
    return lambda i: (i + NZ * shift) % (NX * NZ)


def along_z(shift):
    return lambda i: i // NZ * NZ + (i + shift) % NZ


def on_device(front, test, child, child_group, child_block, inv_leaf, inv_parent, pivot_leaf, pivot_parent):
    row, column = lax.axis_index("frow"), lax.axis_index("fcol")
    leaves = lax.axis_size("fcol")
    blocks = front.shape[0] // BLK
    rank = pivot_leaf.shape[1]

    packed = pack(child, child_group.T, child_block.reshape(1, CBD), pivot_leaf, blocks)
    mine = lax.all_to_all(packed, "fcol", 0, 0, tiled=True)

    own_x, *x_parts, xa, xb, own_z, z1, z3, w1, w3, za, zb = front_products(front, test)
    xa, xb = moved(xa, "fcol", along_x(1)), moved(xb, "fcol", along_x(3))
    za, zb = moved(za, "fcol", along_z(1)), moved(zb, "fcol", along_z(3))
    x_up, x_down, z_up, z_down, mine = relay(x_parts, xa, xb, (z1, z3, w1, w3), za, zb, inv_parent.T, mine)
    other = moved(mine, "frow", lambda i: i ^ 1)
    in_x = [moved(x_up, "fcol", along_x(1)), moved(x_down, "fcol", along_x(3))]
    in_z = [moved(z_up, "fcol", along_z(1)), moved(z_down, "fcol", along_z(3))]

    out_y, own_y, piv_leaf = place(mine, other, blocks)
    in_y = lax.all_to_all(
        out_y, "frow", 0, 0, tiled=True, axis_index_groups=[[2 * i + core for i in range(NY)] for core in range(2)]
    )
    token, piv_leaf = piv_leaf, piv_leaf[:, :rank]

    half = blocks // 2
    *out_x, own_x = partial_sum(sum_x_kernel, own_x, in_x, token, half, [])
    in_x = [moved(v, "fcol", along_z(s)) for s, v in zip((1, 2, 3), out_x)]
    inverse = jax.ShapeDtypeStruct(inv_parent.T.shape, BF16)
    *out_z, own_z, inv_other = partial_sum(sum_z_kernel, own_z, in_z, token, half, [inverse])
    in_z = [moved(v, "fcol", along_x(s)) for s, v in zip((1, 2, 3), out_z)]

    placed = finish([own_x, *in_x], [own_z, *in_z], own_y, in_y, leaves)
    arrived = lax.all_to_all(placed, "fcol", 0, 0, tiled=True)
    count = front.shape[0] // leaves
    samples, interp_leaf, interp_parent, skeleton_parent = tail(
        arrived, inv_leaf.T, inv_parent.T, inv_other, piv_leaf, pivot_parent, count
    )
    return samples, interp_leaf.T, interp_parent.T, skeleton_parent


def solution(mesh):
    both = P(("frow", "fcol"), None)
    return jax.shard_map(
        on_device,
        mesh=mesh,
        in_specs=(P("frow", "fcol"), P("fcol", None), both, both, P(("frow", "fcol")), both, both, both, both),
        out_specs=(both,) * 4,
        check_vma=False,
    )
```

```python
import functools

import jax
import jax.numpy as jnp
from jax import lax
from jax.experimental import pallas as pl
from jax.experimental.pallas import tpu as pltpu
from jax.sharding import PartitionSpec as P

BF16 = jnp.bfloat16
F32 = jnp.float32
BLK = 128
CBD = 8
NX = 4
NZ = 4
NY = 4
UNIT = 32
TOLD = 16
COLS = 128
LOCAL = pl.BlockSpec(memory_space=pltpu.VMEM)
REMAIN = pl.BlockSpec(memory_space=pltpu.HBM)
ANY = pl.BlockSpec(memory_space=pl.ANY)


def params(mebibytes):
    return pltpu.CompilerParams(vmem_limit_bytes=mebibytes * 1024 * 1024)


def cost(flops, moved_bytes):
    return pl.CostEstimate(flops=flops, bytes_accessed=moved_bytes, transcendentals=0)


def place_in_mesh():
    row, column = lax.axis_index("frow"), lax.axis_index("fcol")
    return column // NZ, column % NZ, column, row // 2, row % 2


def remote(value):
    return pltpu.with_memory_space_constraint(value, pltpu.HBM)


def fetch(pairs, sems):
    copies = [pltpu.make_async_copy(src, dst, sems.at[i]) for i, (src, dst) in enumerate(pairs)]
    for copy in copies:
        copy.start()
    return copies


def put_parts(products, stores, out_sems):
    for (ref, out), at, value in products:
        ref[at : at + value.shape[0]] = value.astype(ref.dtype)
        if out is not None:
            span = pl.ds(at, value.shape[0])
            stores.append(pltpu.make_async_copy(ref.at[span], out.at[span], out_sems.at[len(stores)]))
            stores[-1].start()


def part_products(rows_x, rows_z, weights, weights_z, x_targets, z_targets, ready, out_sems):
    half, depth = rows_z.shape[0], rows_z.shape[-1]
    step = half // 2
    stores = []
    for i, target in enumerate(x_targets):
        ready(i)
        product = jnp.dot(rows_x[i].reshape(half * UNIT, depth), weights[...], preferred_element_type=F32)
        product = product.reshape(half, UNIT, NZ * COLS)
        put_parts([(target[t], 0, product[t * step : (t + 1) * step]) for t in range(2)], stores, out_sems)
    for part in range(2):
        ready(len(x_targets) + part)
        rows = rows_z[part * step : (part + 1) * step].reshape(step * BLK, depth)
        product = jnp.dot(rows, weights_z[...], preferred_element_type=F32)
        product = product.reshape(step, NX, UNIT, 2 * COLS)
        for jr in range(NX):
            at = jr % (NX // 2) * half + part * step
            put_parts(
                [
                    (target[jr // (NX // 2)], at, product[:, jr, :, i * COLS : (i + 1) * COLS])
                    for i, target in enumerate(z_targets)
                ],
                stores, out_sems,
            )
    for store in stores:
        store.wait()


def far_kernel(a_hbm, b_hbm, token, xa, xb, za, zb, oz_low, oz_high, near_x, rows_z, turned, turned_z,
               ax, b, bz, sz_low, sz_high, sems, out_sems):
    x, z = place_in_mesh()[:2]
    half = rows_z.shape[0]
    step = half // 2
    pairs = [(b_hbm, b)]
    pairs += [(a_hbm.at[:half, (x + 2) % NX], ax.at[0])]
    pairs += [
        (a_hbm.at[half + i * step : half + (i + 1) * step], rows_z.at[i * step : (i + 1) * step]) for i in range(2)
    ]
    pairs += [(a_hbm.at[:half, (x + s) % NX], near_x.at[i]) for i, s in enumerate((1, 3, 0))]
    loads = [pltpu.make_async_copy(src, dst, sems.at[i]) for i, (src, dst) in enumerate(pairs)]
    for load in loads[:3]:
        load.start()

    def ready(i):
        loads[i + 1].wait()
        if i + 4 < len(loads):
            loads[i + 4].start()

    ready(-1)
    for s in range(NZ):
        piece = b[:, pl.ds(pl.multiple_of((z + s) % NZ * COLS, COLS), COLS)]
        turned[:, s * COLS : (s + 1) * COLS] = piece
        out, at = (bz, (2 - s) // 2 * COLS) if s % 2 == 0 else (turned_z, s // 2 * COLS)
        out[:, at : at + COLS] = piece
    part_products(
        ax, rows_z, turned, bz,
        (((xa, None), (xb, None)),),
        (((za, None), (zb, None)), ((sz_low, oz_low), (sz_high, oz_high))),
        ready, out_sems,
    )
    for load in loads[4:]:
        load.wait()


def near_kernel(near_x, rows_z, turned, turned_z, x1, u1, u3, x3, ox_low, ox_high, z1, w1, w3, z3,
                sx1, su1, su3, sx3, sx_low, sx_high, sz1, sw1, sw3, sz3, out_sems):
    part_products(
        near_x, rows_z, turned, turned_z,
        (((sx1, x1), (su1, u1)), ((su3, u3), (sx3, x3)), ((sx_low, ox_low), (sx_high, ox_high))),
        (((sz1, z1), (sw1, w1)), ((sw3, w3), (sz3, z3))),
        lambda i: None, out_sems,
    )


def far_products(front, test, token):
    blocks, depth, cols = front.shape[0] // BLK, front.shape[1], test.shape[1]
    half = blocks // 2
    x_shape, z_shape = (half // 2, UNIT, cols), (NX // 2 * half, UNIT, COLS)
    sent = [jax.ShapeDtypeStruct(shape, BF16) for shape in (x_shape, x_shape, z_shape, z_shape)]
    kept = [((3, half, UNIT, depth), BF16), ((half, NX, UNIT, depth), BF16), (test.shape, BF16), ((depth, 2 * COLS), BF16)]
    return pl.pallas_call(
        far_kernel,
        out_shape=sent + [pltpu.HBM(z_shape, F32)] * 2 + [pltpu.VMEM(*k) for k in kept],
        in_specs=[REMAIN] * 2 + [ANY],
        out_specs=[LOCAL] * 4 + [REMAIN] * 2 + [LOCAL] * 4,
        scratch_shapes=[
            pltpu.VMEM((1, half, UNIT, depth), BF16),
            pltpu.VMEM(test.shape, BF16),
            pltpu.VMEM((depth, 2 * COLS), BF16),
            *[pltpu.VMEM(z_shape, F32)] * 2,
            pltpu.SemaphoreType.DMA((7,)),
            pltpu.SemaphoreType.DMA((12,)),
        ],
        compiler_params=params(18),
        cost_estimate=cost(front.size * cols, 2 * (front.size + test.size) + 3 * blocks * BLK * cols),
        name="far",
    )(remote(front.reshape(blocks, NX, UNIT, depth)), remote(test), token)


def near_products(near_x, rows_z, turned, turned_z):
    half, cols = rows_z.shape[0], turned.shape[1]
    kinds = (F32, BF16, BF16, F32)
    shapes = [((half // 2, UNIT, cols), t) for t in (*kinds, F32, F32)]
    shapes += [((NX // 2 * half, UNIT, COLS), t) for t in kinds]
    return pl.pallas_call(
        near_kernel,
        out_shape=[pltpu.HBM(*s) for s in shapes],
        in_specs=[LOCAL] * 4,
        out_specs=[REMAIN] * 10,
        scratch_shapes=[*[pltpu.VMEM(*s) for s in shapes], pltpu.SemaphoreType.DMA((22,))],
        compiler_params=params(12),
        cost_estimate=cost(8 * half * BLK * turned.size, 20 * half * BLK * cols),
        name="near",
    )(*[pltpu.with_memory_space_constraint(v, pltpu.VMEM) for v in (near_x, rows_z, turned, turned_z)])


def inverse_tiles(shape):
    return [
        (slice(i, i + UNIT), slice(j, j + COLS))
        for i in range(0, shape[0], UNIT)
        for j in range(0, shape[1], COLS)
    ]


def relay_kernel(hx1, hx3, hu1, hu3, xa, xb, hz1, hz3, hw1, hw3, za, zb, inverse, _,
                 x_up, x_down, z_up, z_down, __, x1, x3, z1, z3, sems):
    nx, nz = x1.shape[0], z1.shape[0]
    copies = fetch(
        [
            (hx1, x1), (hx3, x3), (hz1, z1), (hz3, z3),
            (hu1, x_up.at[nx : 2 * nx]), (hu3, x_down.at[:nx]),
            (hw1, z_up.at[nz : 2 * nz]), (hw3, z_down.at[:nz]),
        ],
        sems,
    )
    for out in (z_up, z_down):
        for i, (rows, columns) in enumerate(inverse_tiles(inverse.shape)):
            out[2 * nz + i] = inverse[rows, columns]
    for copy, own, part, out, at in zip(
        copies, (x1, x3, z1, z3), (xa, xb, za, zb), (x_up, x_down, z_up, z_down), (0, nx, 0, nz)
    ):
        copy.wait()
        out[at : at + own.shape[0]] = (own[...] + part[...].astype(F32)).astype(BF16)
    for copy in copies[4:]:
        copy.wait()


def relay(x_parts, xa, xb, z_parts, za, zb, inverse, mine):
    extra = len(inverse_tiles(inverse.shape))
    nx, nz = xa.shape[0], za.shape[0]
    x_shape, z_shape = (2 * nx, *xa.shape[1:]), (2 * nz + extra, *za.shape[1:])
    shapes = [x_shape, x_shape, z_shape, z_shape, mine.shape]
    return pl.pallas_call(
        relay_kernel,
        out_shape=[jax.ShapeDtypeStruct(shape, BF16) for shape in shapes],
        in_specs=([REMAIN] * 4 + [LOCAL] * 2) * 2 + [LOCAL] * 2,
        out_specs=[LOCAL] * 5,
        scratch_shapes=[
            *[pltpu.VMEM(v.shape, F32) for v in (xa, xb, za, zb)],
            pltpu.SemaphoreType.DMA((8,)),
        ],
        input_output_aliases={13: 4},
        compiler_params=params(8),
        cost_estimate=cost(4 * xa.size, 28 * xa.size),
        name="relay",
    )(*map(remote, x_parts), xa, xb, *map(remote, z_parts), za, zb, inverse, mine)


def sum_x_kernel(low, high, r1, r2, token, to1, to2, to3, keep, own, sems):
    half = low.shape[0]
    copies = fetch([(low, own.at[:half]), (high, own.at[half:])], sems)
    for i, copy in enumerate(copies):
        copy.wait()
        for s, out in ((1, to1), (2, to2), (3, to3), (0, keep)):
            at = (slice(i * half, (i + 1) * half), slice(None), slice(s * COLS, (s + 1) * COLS))
            out[at[0]] = (own[at] + r1[at].astype(F32) + r2[at].astype(F32)).astype(out.dtype)


def sum_z_kernel(low, high, r1, r2, token, to1, to2, to3, keep, inverse, own, sems):
    x, z = place_in_mesh()[:2]
    half = keep.shape[0]
    size = low.shape[0]
    copies = fetch([(low, own.at[:size]), (high, own.at[size:])], sems)
    for copy in copies:
        copy.wait()
    for s, out in ((1, to1), (2, to2), (3, to3), (0, keep)):
        at = pl.ds((x + s) % NX * half, half)
        out[...] = (own[at] + r1[at].astype(F32) + r2[at].astype(F32)).astype(out.dtype)
    for i, (rows, columns) in enumerate(inverse_tiles(inverse.shape)):
        inverse[rows, columns] = lax.select(z % 2 == 0, r2[NX * half + i], r1[NX * half + i])


def partial_sum(kernel, own, arrived, token, half, extra):
    outs = [jax.ShapeDtypeStruct((half, UNIT, COLS), t) for t in (F32, BF16, F32, F32)] + extra
    return pl.pallas_call(
        kernel,
        out_shape=outs,
        in_specs=[REMAIN] * 2 + [LOCAL] * 2 + [ANY],
        out_specs=[LOCAL] * len(outs),
        scratch_shapes=[
            pltpu.VMEM((2 * own[0].shape[0], *own[0].shape[1:]), F32),
            pltpu.SemaphoreType.DMA((2,)),
        ],
        compiler_params=params(8),
        cost_estimate=cost(6 * own[0].size, 28 * own[0].size),
        name=kernel.__name__[:5],
    )(*map(remote, own), *arrived, token)


def pack_kernel(child, group_hbm, block_hbm, pivots_hbm, out, group, block, pivots, facts, local, sems, *, blocks):
    copies = fetch(
        [(group_hbm, group), (block_hbm, block), (pivots_hbm, pivots)]
        + [(child.at[i : i + 2], local.at[i : i + 2]) for i in range(0, CBD, 2)],
        sems,
    )
    facts[...] = jnp.zeros_like(facts)
    for copy in copies[:3]:
        copy.wait()
    facts[0:1, : group.shape[1]] = (group[...] * blocks + block[...]).astype(F32)
    facts[1:2, : pivots.shape[1]] = pivots[...].astype(F32)
    told = facts[...].astype(BF16)
    for i in range(out.shape[0]):
        out[i, CBD * UNIT :] = told
    for i in range(0, CBD, 2):
        copies[3 + i // 2].wait()
        for x in range(NX):
            for z in range(NZ):
                part = local[i : i + 2, x * UNIT : (x + 1) * UNIT, z * COLS : (z + 1) * COLS]
                out[x * NZ + z, i * UNIT : (i + 2) * UNIT] = part.reshape(2 * UNIT, COLS)


def pack(child, group, block, pivots, blocks):
    child = remote(child.reshape(CBD, BLK, child.shape[1]))
    return pl.pallas_call(
        functools.partial(pack_kernel, blocks=blocks),
        out_shape=jax.ShapeDtypeStruct((NX * NZ, CBD * UNIT + TOLD, COLS), BF16),
        in_specs=[REMAIN] * 4,
        out_specs=LOCAL,
        scratch_shapes=[
            *[pltpu.VMEM(v.shape, v.dtype) for v in (group, block, pivots)],
            pltpu.VMEM((TOLD, COLS), F32),
            pltpu.VMEM(child.shape, BF16),
            pltpu.SemaphoreType.DMA((CBD // 2 + 3,)),
        ],
        compiler_params=params(60),
        cost_estimate=cost(0, 4 * child.size),
        name="pack",
    )(child, group, block, pivots)


def place_kernel(mine, other, out, own, pivots, total, facts, told, slots, sems):
    pos = place_in_mesh()
    blocks = out.shape[1]
    sources = mine.shape[0]
    for t, ref in ((0, mine), (1, other)):
        told[t * sources : (t + 1) * sources] = ref[:, CBD * UNIT :].astype(F32)
    dest = told[:, 0].astype(jnp.int32)
    group = dest // blocks
    facts[...] = jnp.where(
        group % 2 == pos[4], group // 2 * blocks + dest % blocks, NY * blocks
    )
    copy = pltpu.make_async_copy(facts, slots, sems.at[0])
    copy.start()
    pivots[...] = told[pl.ds(pos[2] // 2 * 2, 2), 1].astype(jnp.int32)
    total[...] = jnp.zeros_like(total)
    copy.wait()
    for t, ref in ((0, mine), (1, other)):
        def body(i, _, t=t, ref=ref):
            for j in range(CBD):
                at = slots[t * sources + i, j]
                total[at] += ref[i, j * UNIT : (j + 1) * UNIT].astype(F32)
            return _

        lax.fori_loop(0, sources, body, 0)
    keep = pltpu.make_async_copy(total.at[pl.ds(pos[3] * blocks, blocks)], own, sems.at[0])
    keep.start()
    out[...] = total[: NY * blocks].reshape(out.shape).astype(BF16)
    keep.wait()


def place(mine, other, blocks):
    piece = (blocks, UNIT, COLS)
    sources = mine.shape[0]
    return pl.pallas_call(
        place_kernel,
        out_shape=[
            jax.ShapeDtypeStruct((NY, *piece), BF16),
            pltpu.HBM(piece, F32),
            jax.ShapeDtypeStruct((2, COLS), jnp.int32),
        ],
        in_specs=[LOCAL] * 2,
        out_specs=[LOCAL, REMAIN, LOCAL],
        scratch_shapes=[
            pltpu.VMEM((NY * blocks + 1, UNIT, COLS), F32),
            pltpu.VMEM((2 * sources, COLS), jnp.int32),
            pltpu.VMEM((2 * sources, TOLD, COLS), F32),
            pltpu.SMEM((2 * sources, COLS), jnp.int32),
            pltpu.SemaphoreType.DMA((1,)),
        ],
        compiler_params=params(8),
        cost_estimate=cost(16 * mine.size, 8 * mine.size),
        name="place",
    )(mine, other)


def finish_kernel(*refs):
    pos = place_in_mesh()
    fx, fz, held, arrived, out, total, own, sems = refs[:4], refs[4:8], *refs[8:14]
    fetched = fetch([(held, own)], sems)[0]
    half = fx[0].shape[0]
    blocks = 2 * half
    for first, part in ((0, fx), (half, fz)):
        value = part[0][...] + part[1][...] + part[2][...].astype(F32) + part[3][...]
        span = slice(first, first + half)
        if first == 0:
            fetched.wait()
        value = value + own[span]
        for shift in (1, 2, 3):
            value = value + arrived[(pos[3] + shift) % NY, span].astype(F32)
        total[span] = value.astype(BF16)
    units = blocks * NX // out.shape[0]
    for leaf in range(out.shape[0]):
        offset = (pos[0] - units * leaf) % NX
        for slot in range(2):
            unit = units * leaf + offset + NX * slot
            value = total[jnp.minimum(unit // NX, blocks - 1)]
            for dest in (leaf // 2 * 2, leaf // 2 * 2 + 1):
                out[dest, leaf % 2, slot] = value


def finish(fx, fz, own, arrived, leaves):
    blocks = own.shape[0]
    piece = (blocks // 2, UNIT, COLS)
    return pl.pallas_call(
        finish_kernel,
        out_shape=jax.ShapeDtypeStruct((leaves, 2, 2, UNIT, COLS), BF16),
        in_specs=[LOCAL] * 8 + [REMAIN, LOCAL],
        out_specs=LOCAL,
        scratch_shapes=[
            pltpu.VMEM(own.shape, BF16),
            pltpu.VMEM(own.shape, F32),
            pltpu.SemaphoreType.DMA((1,)),
        ],
        compiler_params=params(8),
        cost_estimate=cost(8 * own.size, 30 * own.size),
        name="finish",
    )(*[f.reshape(piece) for f in fx], *[f.reshape(piece) for f in fz], remote(own), arrived)


def across(a, b):
    return lax.dot_general(a, b, (((1,), (1,)), ((), ())), preferred_element_type=F32)


def tail_kernel(arrived, inv_leaf, inv_own, inv_other, piv_leaf, piv_parent,
                samples, interp_leaf, interp_parent, skeleton_parent, rows, stacked):
    pos = place_in_mesh()
    leaf = pos[2]
    units = samples.shape[0] // UNIT
    parity = leaf % 2
    for x in range(NX):
        for z in range(NZ):
            for t in range(2):
                offset = (x - units * (leaf - parity + t)) % NX
                for slot in range(2):
                    rows[t, offset + NX * slot, :, z * COLS : (z + 1) * COLS] = arrived[x * NZ + z, t, slot]
    padded = rows.shape[1] * UNIT
    count = samples.shape[0]
    rank = interp_parent.shape[1]
    leaf_rows = rows[parity].reshape(padded, rows.shape[-1])
    samples[...] = leaf_rows[:count]
    interp_leaf[...] = across(inv_leaf[...], leaf_rows)[:, :count]

    def pick(pivots, source):
        hit = lax.broadcasted_iota(jnp.int32, (source.shape[0], pivots.shape[1]), 0) == pivots
        return lax.dot_general(
            hit.astype(F32).astype(BF16), source, (((0,), (0,)), ((), ())), preferred_element_type=F32
        ).astype(BF16)

    for t in range(2):
        stacked[t] = pick(piv_leaf[t : t + 1], rows[t].reshape(padded, rows.shape[-1]))
    both = stacked[...].reshape(2 * rank, stacked.shape[-1])
    skeleton_parent[...] = pick(piv_parent[...], both)
    depth = inv_own.shape[1]
    skeleton = stacked[parity]
    even = lax.select(parity == 0, inv_own[...], inv_other[...])
    odd = lax.select(parity == 0, inv_other[...], inv_own[...])
    interp_parent[...] = across(even, skeleton[:, :depth]) + across(odd, skeleton[:, depth:])


def tail(arrived, inv_leaf, inv_own, inv_other, piv_leaf, piv_parent, count):
    rank, cols = inv_leaf.shape
    padded = 2 * NX * UNIT
    args = (arrived, inv_leaf, inv_own, inv_other, piv_leaf, piv_parent)
    outs = [
        jax.ShapeDtypeStruct((count, cols), BF16),
        jax.ShapeDtypeStruct((rank, count), F32),
        jax.ShapeDtypeStruct((inv_own.shape[0], rank), F32),
        jax.ShapeDtypeStruct((piv_parent.shape[1], cols), BF16),
    ]
    return pl.pallas_call(
        tail_kernel,
        out_shape=outs,
        in_specs=[LOCAL] * len(args),
        out_specs=[LOCAL] * len(outs),
        scratch_shapes=[
            pltpu.VMEM((2, padded // UNIT, UNIT, cols), BF16),
            pltpu.VMEM((2, rank, cols), BF16),
        ],
        compiler_params=params(8),
        cost_estimate=cost(6 * padded * rank * cols, 6 * padded * cols),
        name="tail",
    )(*args)


def moved(x, axis, to):
    return lax.ppermute(x, axis, [(i, to(i)) for i in range(lax.axis_size(axis))])


def along_x(shift):
    return lambda i: (i + NZ * shift) % (NX * NZ)


def along_z(shift):
    return lambda i: i // NZ * NZ + (i + shift) % NZ


def on_device(front, test, child, child_group, child_block, inv_leaf, inv_parent, pivot_leaf, pivot_parent):
    row, column = lax.axis_index("frow"), lax.axis_index("fcol")
    leaves = lax.axis_size("fcol")
    blocks = front.shape[0] // BLK
    rank = pivot_leaf.shape[1]

    packed = pack(child, child_group.T, child_block.reshape(1, CBD), pivot_leaf, blocks)
    mine = lax.all_to_all(packed, "fcol", 0, 0, tiled=True)

    xa, xb, za, zb, z_low, z_high, near_x, rows_z, turned, turned_z = far_products(front, test, packed)
    xa, xb = moved(xa, "fcol", along_x(1)), moved(xb, "fcol", along_x(3))
    za, zb = moved(za, "fcol", along_z(1)), moved(zb, "fcol", along_z(3))
    x1, u1, u3, x3, x_low, x_high, z1, w1, w3, z3 = near_products(near_x, rows_z, turned, turned_z)
    own_x, own_z = (x_low, x_high), (z_low, z_high)
    x_up, x_down, z_up, z_down, mine = relay(
        (x1, x3, u1, u3), xa, xb, (z1, z3, w1, w3), za, zb, inv_parent.T, mine
    )
    other = moved(mine, "frow", lambda i: i ^ 1)
    in_x = [moved(x_up, "fcol", along_x(1)), moved(x_down, "fcol", along_x(3))]
    in_z = [moved(z_up, "fcol", along_z(1)), moved(z_down, "fcol", along_z(3))]

    out_y, own_y, piv_leaf = place(mine, other, blocks)
    in_y = lax.all_to_all(
        out_y, "frow", 0, 0, tiled=True, axis_index_groups=[[2 * i + core for i in range(NY)] for core in range(2)]
    )
    token, piv_leaf = piv_leaf, piv_leaf[:, :rank]

    half = blocks // 2
    *out_x, own_x = partial_sum(sum_x_kernel, own_x, in_x, token, half, [])
    in_x = [moved(v, "fcol", along_z(s)) for s, v in zip((1, 2, 3), out_x)]
    inverse = jax.ShapeDtypeStruct(inv_parent.T.shape, BF16)
    *out_z, own_z, inv_other = partial_sum(sum_z_kernel, own_z, in_z, token, half, [inverse])
    in_z = [moved(v, "fcol", along_x(s)) for s, v in zip((1, 2, 3), out_z)]

    placed = finish([own_x, *in_x], [own_z, *in_z], own_y, in_y, leaves)
    arrived = lax.all_to_all(placed, "fcol", 0, 0, tiled=True)
    count = front.shape[0] // leaves
    samples, interp_leaf, interp_parent, skeleton_parent = tail(
        arrived, inv_leaf.T, inv_parent.T, inv_other, piv_leaf, pivot_parent, count
    )
    return samples, interp_leaf.T, interp_parent.T, skeleton_parent


def solution(mesh):
    both = P(("frow", "fcol"), None)
    return jax.shard_map(
        on_device,
        mesh=mesh,
        in_specs=(P("frow", "fcol"), P("fcol", None), both, both, P(("frow", "fcol")), both, both, both, both),
        out_specs=(both,) * 4,
        check_vma=False,
    )
```

```python
import functools

import jax
import jax.numpy as jnp
from jax import lax
from jax.experimental import pallas as pl
from jax.experimental.pallas import tpu as pltpu
from jax.sharding import PartitionSpec as P

BF16 = jnp.bfloat16
F32 = jnp.float32
BLK = 128
CBD = 8
NX = 4
NZ = 4
NY = 4
UNIT = 32
TOLD = 16
COLS = 128
LOCAL = pl.BlockSpec(memory_space=pltpu.VMEM)
REMAIN = pl.BlockSpec(memory_space=pltpu.HBM)
ANY = pl.BlockSpec(memory_space=pl.ANY)


def params(mebibytes):
    return pltpu.CompilerParams(vmem_limit_bytes=mebibytes * 1024 * 1024)


def cost(flops, moved_bytes):
    return pl.CostEstimate(flops=flops, bytes_accessed=moved_bytes, transcendentals=0)


def place_in_mesh():
    row, column = lax.axis_index("frow"), lax.axis_index("fcol")
    return column // NZ, column % NZ, column, row // 2, row % 2


def remote(value):
    return pltpu.with_memory_space_constraint(value, pltpu.HBM)


def fetch(pairs, sems):
    copies = [pltpu.make_async_copy(src, dst, sems.at[i]) for i, (src, dst) in enumerate(pairs)]
    for copy in copies:
        copy.start()
    return copies


def put_parts(products, stores, out_sems):
    for (ref, out), at, value in products:
        ref[at : at + value.shape[0]] = value.astype(ref.dtype)
        if out is not None:
            span = pl.ds(at, value.shape[0])
            stores.append(pltpu.make_async_copy(ref.at[span], out.at[span], out_sems.at[len(stores)]))
            stores[-1].start()


def part_products(rows_x, rows_z, weights, weights_z, x_targets, z_targets, ready, out_sems):
    half, depth = rows_z.shape[0], rows_z.shape[-1]
    step = half // 2
    stores = []
    for i, target in enumerate(x_targets):
        ready(i)
        product = jnp.dot(rows_x[i].reshape(half * UNIT, depth), weights[...], preferred_element_type=F32)
        product = product.reshape(half, UNIT, NZ * COLS)
        put_parts([(target[t], 0, product[t * step : (t + 1) * step]) for t in range(2)], stores, out_sems)
    for part in range(2):
        ready(len(x_targets) + part)
        rows = rows_z[part * step : (part + 1) * step].reshape(step * BLK, depth)
        product = jnp.dot(rows, weights_z[...], preferred_element_type=F32)
        product = product.reshape(step, NX, UNIT, 2 * COLS)
        for jr in range(NX):
            at = jr % (NX // 2) * half + part * step
            put_parts(
                [
                    (target[jr // (NX // 2)], at, product[:, jr, :, i * COLS : (i + 1) * COLS])
                    for i, target in enumerate(z_targets)
                ],
                stores, out_sems,
            )
    for store in stores:
        store.wait()


def far_kernel(a_hbm, b_hbm, token, xa, xb, za, zb, oz_low, oz_high, near_x, rows_z, turned, turned_z,
               ax, b, bz, sz_low, sz_high, sems, out_sems):
    x, z = place_in_mesh()[:2]
    half = rows_z.shape[0]
    step = half // 2
    pairs = [(b_hbm, b)]
    pairs += [(a_hbm.at[:half, (x + 2) % NX], ax.at[0])]
    pairs += [
        (a_hbm.at[half + i * step : half + (i + 1) * step], rows_z.at[i * step : (i + 1) * step]) for i in range(2)
    ]
    pairs += [(a_hbm.at[:half, (x + s) % NX], near_x.at[i]) for i, s in enumerate((1, 3, 0))]
    loads = [pltpu.make_async_copy(src, dst, sems.at[i]) for i, (src, dst) in enumerate(pairs)]
    for load in loads[:3]:
        load.start()

    def ready(i):
        loads[i + 1].wait()
        if i + 4 < len(loads):
            loads[i + 4].start()

    ready(-1)
    for s in range(NZ):
        piece = b[:, pl.ds(pl.multiple_of((z + s) % NZ * COLS, COLS), COLS)]
        turned[:, s * COLS : (s + 1) * COLS] = piece
        out, at = (bz, (2 - s) // 2 * COLS) if s % 2 == 0 else (turned_z, s // 2 * COLS)
        out[:, at : at + COLS] = piece
    part_products(
        ax, rows_z, turned, bz,
        (((xa, None), (xb, None)),),
        (((za, None), (zb, None)), ((sz_low, oz_low), (sz_high, oz_high))),
        ready, out_sems,
    )
    for load in loads[4:]:
        load.wait()


def near_kernel(near_x, rows_z, turned, turned_z, x1, u1, u3, x3, ox_low, ox_high, z1, w1, w3, z3,
                sx1, su1, su3, sx3, sx_low, sx_high, sz1, sw1, sw3, sz3, out_sems):
    part_products(
        near_x, rows_z, turned, turned_z,
        (((sx1, x1), (su1, u1)), ((su3, u3), (sx3, x3)), ((sx_low, ox_low), (sx_high, ox_high))),
        (((sz1, z1), (sw1, w1)), ((sw3, w3), (sz3, z3))),
        lambda i: None, out_sems,
    )


def far_products(front, test, token):
    blocks, depth, cols = front.shape[0] // BLK, front.shape[1], test.shape[1]
    half = blocks // 2
    x_shape, z_shape = (half // 2, UNIT, cols), (NX // 2 * half, UNIT, COLS)
    sent = [jax.ShapeDtypeStruct(shape, BF16) for shape in (x_shape, x_shape, z_shape, z_shape)]
    kept = [((3, half, UNIT, depth), BF16), ((half, NX, UNIT, depth), BF16), (test.shape, BF16), ((depth, 2 * COLS), BF16)]
    return pl.pallas_call(
        far_kernel,
        out_shape=sent + [pltpu.HBM(z_shape, F32)] * 2 + [pltpu.VMEM(*k) for k in kept],
        in_specs=[REMAIN] * 2 + [ANY],
        out_specs=[LOCAL] * 4 + [REMAIN] * 2 + [LOCAL] * 4,
        scratch_shapes=[
            pltpu.VMEM((1, half, UNIT, depth), BF16),
            pltpu.VMEM(test.shape, BF16),
            pltpu.VMEM((depth, 2 * COLS), BF16),
            *[pltpu.VMEM(z_shape, F32)] * 2,
            pltpu.SemaphoreType.DMA((7,)),
            pltpu.SemaphoreType.DMA((12,)),
        ],
        compiler_params=params(18),
        cost_estimate=cost(front.size * cols, 2 * (front.size + test.size) + 3 * blocks * BLK * cols),
        name="far",
    )(remote(front.reshape(blocks, NX, UNIT, depth)), remote(test), token)


def near_products(near_x, rows_z, turned, turned_z):
    half, cols = rows_z.shape[0], turned.shape[1]
    kinds = (F32, BF16, BF16, F32)
    shapes = [((half // 2, UNIT, cols), t) for t in (*kinds, F32, F32)]
    shapes += [((NX // 2 * half, UNIT, COLS), t) for t in kinds]
    return pl.pallas_call(
        near_kernel,
        out_shape=[pltpu.HBM(*s) for s in shapes],
        in_specs=[LOCAL] * 4,
        out_specs=[REMAIN] * 10,
        scratch_shapes=[*[pltpu.VMEM(*s) for s in shapes], pltpu.SemaphoreType.DMA((22,))],
        compiler_params=params(12),
        cost_estimate=cost(8 * half * BLK * turned.size, 20 * half * BLK * cols),
        name="near",
    )(*[pltpu.with_memory_space_constraint(v, pltpu.VMEM) for v in (near_x, rows_z, turned, turned_z)])


def inverse_tiles(shape):
    return [
        (slice(i, i + UNIT), slice(j, j + COLS))
        for i in range(0, shape[0], UNIT)
        for j in range(0, shape[1], COLS)
    ]


def relay_kernel(hx1, hx3, hu1, hu3, xa, xb, hz1, hz3, hw1, hw3, za, zb, inverse, _,
                 x_up, x_down, z_up, z_down, __, x1, x3, z1, z3, sems):
    nx, nz = x1.shape[0], z1.shape[0]
    copies = fetch(
        [
            (hx1, x1), (hx3, x3), (hz1, z1), (hz3, z3),
            (hu1, x_up.at[nx : 2 * nx]), (hu3, x_down.at[:nx]),
            (hw1, z_up.at[nz : 2 * nz]), (hw3, z_down.at[:nz]),
        ],
        sems,
    )
    for out in (z_up, z_down):
        for i, (rows, columns) in enumerate(inverse_tiles(inverse.shape)):
            out[2 * nz + i] = inverse[rows, columns]
    for copy, own, part, out, at in zip(
        copies, (x1, x3, z1, z3), (xa, xb, za, zb), (x_up, x_down, z_up, z_down), (0, nx, 0, nz)
    ):
        copy.wait()
        out[at : at + own.shape[0]] = (own[...] + part[...].astype(F32)).astype(BF16)
    for copy in copies[4:]:
        copy.wait()


def relay(x_parts, xa, xb, z_parts, za, zb, inverse, mine):
    extra = len(inverse_tiles(inverse.shape))
    nx, nz = xa.shape[0], za.shape[0]
    x_shape, z_shape = (2 * nx, *xa.shape[1:]), (2 * nz + extra, *za.shape[1:])
    shapes = [x_shape, x_shape, z_shape, z_shape, mine.shape]
    return pl.pallas_call(
        relay_kernel,
        out_shape=[jax.ShapeDtypeStruct(shape, BF16) for shape in shapes],
        in_specs=([REMAIN] * 4 + [LOCAL] * 2) * 2 + [LOCAL] * 2,
        out_specs=[LOCAL] * 5,
        scratch_shapes=[
            *[pltpu.VMEM(v.shape, F32) for v in (xa, xb, za, zb)],
            pltpu.SemaphoreType.DMA((8,)),
        ],
        input_output_aliases={13: 4},
        compiler_params=params(8),
        cost_estimate=cost(4 * xa.size, 28 * xa.size),
        name="relay",
    )(*map(remote, x_parts), xa, xb, *map(remote, z_parts), za, zb, inverse, mine)


def sum_x_kernel(low, high, r1, r2, token, to1, to2, to3, keep, own, sems):
    half = low.shape[0]
    copies = fetch([(low, own.at[:half]), (high, own.at[half:])], sems)
    for i, copy in enumerate(copies):
        copy.wait()
        for s, out in ((1, to1), (2, to2), (3, to3), (0, keep)):
            at = (slice(i * half, (i + 1) * half), slice(None), slice(s * COLS, (s + 1) * COLS))
            out[at[0]] = (own[at] + r1[at].astype(F32) + r2[at].astype(F32)).astype(out.dtype)


def sum_z_kernel(low, high, r1, r2, token, to1, to2, to3, keep, inverse, own, sems):
    x, z = place_in_mesh()[:2]
    half = keep.shape[0]
    size = low.shape[0]
    copies = fetch([(low, own.at[:size]), (high, own.at[size:])], sems)
    for copy in copies:
        copy.wait()
    for s, out in ((1, to1), (2, to2), (3, to3), (0, keep)):
        at = pl.ds((x + s) % NX * half, half)
        out[...] = (own[at] + r1[at].astype(F32) + r2[at].astype(F32)).astype(out.dtype)
    for i, (rows, columns) in enumerate(inverse_tiles(inverse.shape)):
        inverse[rows, columns] = lax.select(z % 2 == 0, r2[NX * half + i], r1[NX * half + i])


def partial_sum(kernel, own, arrived, token, half, extra):
    outs = [jax.ShapeDtypeStruct((half, UNIT, COLS), t) for t in (F32, BF16, F32, F32)] + extra
    return pl.pallas_call(
        kernel,
        out_shape=outs,
        in_specs=[REMAIN] * 2 + [LOCAL] * 2 + [ANY],
        out_specs=[LOCAL] * len(outs),
        scratch_shapes=[
            pltpu.VMEM((2 * own[0].shape[0], *own[0].shape[1:]), F32),
            pltpu.SemaphoreType.DMA((2,)),
        ],
        compiler_params=params(8),
        cost_estimate=cost(6 * own[0].size, 28 * own[0].size),
        name=kernel.__name__[:5],
    )(*map(remote, own), *arrived, token)


def pack_kernel(child, group_hbm, block_hbm, pivots_hbm, out, group, block, pivots, facts, local, sems, *, blocks):
    copies = fetch(
        [(group_hbm, group), (block_hbm, block), (pivots_hbm, pivots)]
        + [(child.at[i : i + 2], local.at[i : i + 2]) for i in range(0, CBD, 2)],
        sems,
    )
    facts[...] = jnp.zeros_like(facts)
    for copy in copies[:3]:
        copy.wait()
    facts[0:1, : group.shape[1]] = (group[...] * blocks + block[...]).astype(F32)
    facts[1:2, : pivots.shape[1]] = pivots[...].astype(F32)
    told = facts[...].astype(BF16)
    for i in range(out.shape[0]):
        out[i, CBD * UNIT :] = told
    for i in range(0, CBD, 2):
        copies[3 + i // 2].wait()
        for x in range(NX):
            for z in range(NZ):
                part = local[i : i + 2, x * UNIT : (x + 1) * UNIT, z * COLS : (z + 1) * COLS]
                out[x * NZ + z, i * UNIT : (i + 2) * UNIT] = part.reshape(2 * UNIT, COLS)


def pack(child, group, block, pivots, blocks):
    child = remote(child.reshape(CBD, BLK, child.shape[1]))
    return pl.pallas_call(
        functools.partial(pack_kernel, blocks=blocks),
        out_shape=jax.ShapeDtypeStruct((NX * NZ, CBD * UNIT + TOLD, COLS), BF16),
        in_specs=[REMAIN] * 4,
        out_specs=LOCAL,
        scratch_shapes=[
            *[pltpu.VMEM(v.shape, v.dtype) for v in (group, block, pivots)],
            pltpu.VMEM((TOLD, COLS), F32),
            pltpu.VMEM(child.shape, BF16),
            pltpu.SemaphoreType.DMA((CBD // 2 + 3,)),
        ],
        compiler_params=params(60),
        cost_estimate=cost(0, 4 * child.size),
        name="pack",
    )(child, group, block, pivots)


def place_kernel(mine, other, out, own, pivots, total, kept, facts, told, slots, sems):
    pos = place_in_mesh()
    blocks = out.shape[1]
    sources = mine.shape[0]
    for t, ref in ((0, mine), (1, other)):
        told[t * sources : (t + 1) * sources] = ref[:, CBD * UNIT :].astype(F32)
    dest = told[:, 0].astype(jnp.int32)
    group = dest // blocks
    facts[...] = jnp.where(
        group % 2 == pos[4], group // 2 * blocks + dest % blocks, NY * blocks
    )
    copy = pltpu.make_async_copy(facts, slots, sems.at[0])
    copy.start()
    pivots[...] = told[pl.ds(pos[2] // 2 * 2, 2), 1].astype(jnp.int32)
    total[...] = jnp.zeros_like(total)
    copy.wait()

    def body(i, carry):
        for j in range(CBD):
            for t, ref in ((0, mine), (1, other)):
                total[t, slots[t * sources + i, j]] += ref[i, j * UNIT : (j + 1) * UNIT].astype(F32)
        return carry

    lax.fori_loop(0, sources, body, 0)
    span = pl.ds(pos[3] * blocks, blocks)
    kept[...] = total[0, span] + total[1, span]
    keep = pltpu.make_async_copy(kept, own, sems.at[0])
    keep.start()
    places = NY * blocks
    out[...] = (total[0, :places] + total[1, :places]).reshape(out.shape).astype(BF16)
    keep.wait()


def place(mine, other, blocks):
    piece = (blocks, UNIT, COLS)
    sources = mine.shape[0]
    return pl.pallas_call(
        place_kernel,
        out_shape=[
            jax.ShapeDtypeStruct((NY, *piece), BF16),
            pltpu.HBM(piece, F32),
            jax.ShapeDtypeStruct((2, COLS), jnp.int32),
        ],
        in_specs=[LOCAL] * 2,
        out_specs=[LOCAL, REMAIN, LOCAL],
        scratch_shapes=[
            pltpu.VMEM((2, NY * blocks + 1, UNIT, COLS), F32),
            pltpu.VMEM(piece, F32),
            pltpu.VMEM((2 * sources, COLS), jnp.int32),
            pltpu.VMEM((2 * sources, TOLD, COLS), F32),
            pltpu.SMEM((2 * sources, COLS), jnp.int32),
            pltpu.SemaphoreType.DMA((1,)),
        ],
        compiler_params=params(8),
        cost_estimate=cost(16 * mine.size, 8 * mine.size),
        name="place",
    )(mine, other)


def finish_kernel(*refs):
    pos = place_in_mesh()
    fx, fz, held, arrived, out, total, own, sems = refs[:4], refs[4:8], *refs[8:14]
    fetched = fetch([(held, own)], sems)[0]
    half = fx[0].shape[0]
    blocks = 2 * half
    for first, part in ((0, fx), (half, fz)):
        value = part[0][...] + part[1][...] + part[2][...].astype(F32) + part[3][...]
        span = slice(first, first + half)
        if first == 0:
            fetched.wait()
        value = value + own[span]
        for shift in (1, 2, 3):
            value = value + arrived[(pos[3] + shift) % NY, span].astype(F32)
        total[span] = value.astype(BF16)
    units = blocks * NX // out.shape[0]
    for leaf in range(out.shape[0]):
        offset = (pos[0] - units * leaf) % NX
        for slot in range(2):
            unit = units * leaf + offset + NX * slot
            value = total[jnp.minimum(unit // NX, blocks - 1)]
            for dest in (leaf // 2 * 2, leaf // 2 * 2 + 1):
                out[dest, leaf % 2, slot] = value


def finish(fx, fz, own, arrived, leaves):
    blocks = own.shape[0]
    piece = (blocks // 2, UNIT, COLS)
    return pl.pallas_call(
        finish_kernel,
        out_shape=jax.ShapeDtypeStruct((leaves, 2, 2, UNIT, COLS), BF16),
        in_specs=[LOCAL] * 8 + [REMAIN, LOCAL],
        out_specs=LOCAL,
        scratch_shapes=[
            pltpu.VMEM(own.shape, BF16),
            pltpu.VMEM(own.shape, F32),
            pltpu.SemaphoreType.DMA((1,)),
        ],
        compiler_params=params(8),
        cost_estimate=cost(8 * own.size, 30 * own.size),
        name="finish",
    )(*[f.reshape(piece) for f in fx], *[f.reshape(piece) for f in fz], remote(own), arrived)


def across(a, b):
    return lax.dot_general(a, b, (((1,), (1,)), ((), ())), preferred_element_type=F32)


def tail_kernel(arrived, inv_leaf, inv_own, inv_other, piv_leaf, piv_parent,
                samples, interp_leaf, interp_parent, skeleton_parent, rows, stacked):
    pos = place_in_mesh()
    leaf = pos[2]
    units = samples.shape[0] // UNIT
    parity = leaf % 2
    for x in range(NX):
        for z in range(NZ):
            for t in range(2):
                offset = (x - units * (leaf - parity + t)) % NX
                for slot in range(2):
                    rows[t, offset + NX * slot, :, z * COLS : (z + 1) * COLS] = arrived[x * NZ + z, t, slot]
    padded = rows.shape[1] * UNIT
    count = samples.shape[0]
    rank = interp_parent.shape[1]
    leaf_rows = rows[parity].reshape(padded, rows.shape[-1])
    samples[...] = leaf_rows[:count]
    interp_leaf[...] = across(inv_leaf[...], leaf_rows)[:, :count]

    def pick(pivots, source):
        hit = lax.broadcasted_iota(jnp.int32, (source.shape[0], pivots.shape[1]), 0) == pivots
        return lax.dot_general(
            hit.astype(F32).astype(BF16), source, (((0,), (0,)), ((), ())), preferred_element_type=F32
        ).astype(BF16)

    for t in range(2):
        stacked[t] = pick(piv_leaf[t : t + 1], rows[t].reshape(padded, rows.shape[-1]))
    both = stacked[...].reshape(2 * rank, stacked.shape[-1])
    skeleton_parent[...] = pick(piv_parent[...], both)
    depth = inv_own.shape[1]
    skeleton = stacked[parity]
    even = lax.select(parity == 0, inv_own[...], inv_other[...])
    odd = lax.select(parity == 0, inv_other[...], inv_own[...])
    interp_parent[...] = across(even, skeleton[:, :depth]) + across(odd, skeleton[:, depth:])


def tail(arrived, inv_leaf, inv_own, inv_other, piv_leaf, piv_parent, count):
    rank, cols = inv_leaf.shape
    padded = 2 * NX * UNIT
    args = (arrived, inv_leaf, inv_own, inv_other, piv_leaf, piv_parent)
    outs = [
        jax.ShapeDtypeStruct((count, cols), BF16),
        jax.ShapeDtypeStruct((rank, count), F32),
        jax.ShapeDtypeStruct((inv_own.shape[0], rank), F32),
        jax.ShapeDtypeStruct((piv_parent.shape[1], cols), BF16),
    ]
    return pl.pallas_call(
        tail_kernel,
        out_shape=outs,
        in_specs=[LOCAL] * len(args),
        out_specs=[LOCAL] * len(outs),
        scratch_shapes=[
            pltpu.VMEM((2, padded // UNIT, UNIT, cols), BF16),
            pltpu.VMEM((2, rank, cols), BF16),
        ],
        compiler_params=params(8),
        cost_estimate=cost(6 * padded * rank * cols, 6 * padded * cols),
        name="tail",
    )(*args)


def moved(x, axis, to):
    return lax.ppermute(x, axis, [(i, to(i)) for i in range(lax.axis_size(axis))])


def along_x(shift):
    return lambda i: (i + NZ * shift) % (NX * NZ)


def along_z(shift):
    return lambda i: i // NZ * NZ + (i + shift) % NZ


def on_device(front, test, child, child_group, child_block, inv_leaf, inv_parent, pivot_leaf, pivot_parent):
    row, column = lax.axis_index("frow"), lax.axis_index("fcol")
    leaves = lax.axis_size("fcol")
    blocks = front.shape[0] // BLK
    rank = pivot_leaf.shape[1]

    packed = pack(child, child_group.T, child_block.reshape(1, CBD), pivot_leaf, blocks)
    mine = lax.all_to_all(packed, "fcol", 0, 0, tiled=True)

    xa, xb, za, zb, z_low, z_high, near_x, rows_z, turned, turned_z = far_products(front, test, packed)
    xa, xb = moved(xa, "fcol", along_x(1)), moved(xb, "fcol", along_x(3))
    za, zb = moved(za, "fcol", along_z(1)), moved(zb, "fcol", along_z(3))
    x1, u1, u3, x3, x_low, x_high, z1, w1, w3, z3 = near_products(near_x, rows_z, turned, turned_z)
    own_x, own_z = (x_low, x_high), (z_low, z_high)
    x_up, x_down, z_up, z_down, mine = relay(
        (x1, x3, u1, u3), xa, xb, (z1, z3, w1, w3), za, zb, inv_parent.T, mine
    )
    other = moved(mine, "frow", lambda i: i ^ 1)
    in_x = [moved(x_up, "fcol", along_x(1)), moved(x_down, "fcol", along_x(3))]
    in_z = [moved(z_up, "fcol", along_z(1)), moved(z_down, "fcol", along_z(3))]

    out_y, own_y, piv_leaf = place(mine, other, blocks)
    in_y = lax.all_to_all(
        out_y, "frow", 0, 0, tiled=True, axis_index_groups=[[2 * i + core for i in range(NY)] for core in range(2)]
    )
    token, piv_leaf = piv_leaf, piv_leaf[:, :rank]

    half = blocks // 2
    *out_x, own_x = partial_sum(sum_x_kernel, own_x, in_x, token, half, [])
    in_x = [moved(v, "fcol", along_z(s)) for s, v in zip((1, 2, 3), out_x)]
    inverse = jax.ShapeDtypeStruct(inv_parent.T.shape, BF16)
    *out_z, own_z, inv_other = partial_sum(sum_z_kernel, own_z, in_z, token, half, [inverse])
    in_z = [moved(v, "fcol", along_x(s)) for s, v in zip((1, 2, 3), out_z)]

    placed = finish([own_x, *in_x], [own_z, *in_z], own_y, in_y, leaves)
    arrived = lax.all_to_all(placed, "fcol", 0, 0, tiled=True)
    count = front.shape[0] // leaves
    samples, interp_leaf, interp_parent, skeleton_parent = tail(
        arrived, inv_leaf.T, inv_parent.T, inv_other, piv_leaf, pivot_parent, count
    )
    return samples, interp_leaf.T, interp_parent.T, skeleton_parent


def solution(mesh):
    both = P(("frow", "fcol"), None)
    return jax.shard_map(
        on_device,
        mesh=mesh,
        in_specs=(P("frow", "fcol"), P("fcol", None), both, both, P(("frow", "fcol")), both, both, both, both),
        out_specs=(both,) * 4,
        check_vma=False,
    )
```
